32 devices in a mesh: frag: 2 (over x), pair: 16 (over z, y, core).
Axes of the slice: x: 2, y: 2, z: 4, core: 2. Of those that a mesh axis runs over, the one named last changes fastest.
Arguments:
- amplitudes: float32 [256, 4096], P(('frag', 'pair')), parts along dimension 0, may hold values from -6 to 6
- integrals: float32 [256, 4096], P(('frag', 'pair')), parts along dimension 0, may hold values from -6 to 6
- virtual: float32 [256, 64], P(('frag', 'pair')), parts along dimension 0, may hold values from 0.3 to 3
- occupied: float32 [256], P(('frag', 'pair')), parts along dimension 0, may hold values from -2 to -0.4
- coupling: float32 [256, 16], P(('frag', 'pair')), parts along dimension 0, may hold values from -3 to 3
- degree: int32 [256], P(('frag', 'pair')), parts along dimension 0, may hold values from 1 to 16, as said below
- position: int32 [256, 16], P(('frag', 'pair')), parts along dimension 0, may hold values from 0 to 31
- request: int32 [32, 32], P(('frag', 'pair')), parts along dimension 0, may hold values from 0 to 7
- pnos: bfloat16 [256, 64, 256], P(('frag', 'pair')), parts along dimension 0, may hold values from -1.5 to 1.5
- domains: int32 [256, 16], P(('frag', 'pair')), parts along dimension 0, may hold values from 0 to 31, as said below
Outputs:
- new_amplitudes: float32 [256, 4096], P(('frag', 'pair')), parts along dimension 0
- residual: float32 [256, 4096], P(('frag', 'pair')), parts along dimension 0
The draws below stay inside these ranges and needn't reach their ends.
There are 2 independent parts, one for each index of `frag`. The reference program is written for one: setup_inputs(seed, part) draws one part's arguments, and reference() takes and returns one part's arrays. A program takes and returns all parts, laid end to end along the dimension named above; each array names one. Nothing has to cross between parts.
Inputs may be any that keep to these rules, and one draw needn't show every extreme that they name: `degree`: every pair has at least one coupling, and some pair has 16. `domains`: the 16 atoms of a pair's domain are distinct.
All inputs are finite; a program needn't handle non-finite values.
Results may differ from the reference program's by a relative error of at most 0.0003.
Values may be sent and summed in bfloat16 or wider, within the bound.
No kernel may reach another device: no remote copies, remote signals or barrier semaphores. Data moves between devices by JAX's collectives and lax.ppermute only.
A program may use at most 128 MiB of HBM per device.

```python
import math
import jax
import jax.numpy as jnp
from jax import lax

P_SIZE = 64
NA = 16
B = 16
KMAX = 16
CAP = 2
SWEEPS = 2
SLOTS_DEV = 8
SLOTS = 128
DOM = 256
ATOMS = 32
N_PAIR = 16


def draw_degree(key, part):
    key = jax.random.fold_in(key, 11)
    key_caps, key_top, key_raw, key_pick = jax.random.split(key, 4)
    device_count = SLOTS // SLOTS_DEV
    caps = jax.random.randint(key_caps, (device_count,), KMAX // 4, KMAX + 1)
    chosen = jax.random.randint(key_top, (), 0, device_count)
    caps = jnp.where(jnp.arange(device_count) == chosen, KMAX, caps)
    raw_values = jax.random.randint(key_raw, (device_count, SLOTS_DEV), 0, 1 << 20)
    counts = 1 + raw_values % caps[:, None]
    pick_slot = jax.random.randint(key_pick, (device_count,), 0, SLOTS_DEV)
    counts = jnp.where(jnp.arange(SLOTS_DEV)[None, :] == pick_slot[:, None], caps[:, None], counts)
    return counts.reshape(SLOTS).astype(jnp.int32)


def draw_domains(key, part):
    key = jax.random.fold_in(key, 7)
    row_keys = jax.random.split(key, SLOTS)

    def one_domain(row_key):
        return jax.random.permutation(row_key, ATOMS)[:NA]
    return jax.vmap(one_domain)(row_keys).astype(jnp.int32)


def plant(result, key, low, high):
    place = [jax.random.randint(jax.random.fold_in(key, axis), (), 0, length) for axis, length in enumerate(result.shape)]
    main_axis = result.shape.index(max(result.shape))
    beside = place[:main_axis] + [(place[main_axis] + 1) % result.shape[main_axis]] + place[main_axis + 1:]
    return result.at[tuple(place)].set(low).at[tuple(beside)].set(high)


def level_of(key, dims, cuts, smallest, top_value):
    loudness = 1.0
    for dim, parts in cuts:
        steps = jax.random.uniform(jax.random.fold_in(jax.random.fold_in(key, 6), dim), (parts,), jnp.float32, smallest / len(cuts), top_value / len(cuts))
        loudness = loudness * jnp.repeat(jnp.exp(steps), dims[dim] // parts).reshape((-1,) + (1,) * (len(dims) - 1 - dim))
    return loudness


def centred(key, dims, deviation, limit, cuts=(), kind=jnp.bfloat16):
    values = deviation * jax.random.normal(key, dims, jnp.float32)
    if cuts:
        values = values * level_of(key, dims, cuts, -0.22, 0.18)
    return jnp.clip(values, -limit, limit).astype(kind)


def setup_inputs(seed: int = 0, part: int = 0) -> dict:
    arg_keys = jax.random.split(jax.random.key(seed), 11)
    part_splits = jax.random.split(jax.random.fold_in(arg_keys[10], part), 11)
    return {
        "amplitudes": centred(part_splits[0], (SLOTS, P_SIZE * P_SIZE), 1.0, 6.0, ((0, 16),), jnp.float32),
        "integrals": centred(part_splits[1], (SLOTS, P_SIZE * P_SIZE), 1.0, 6.0, ((0, 16),), jnp.float32),
        "virtual": jnp.clip(jnp.exp(math.log(3.0) - 2.3025851 * jax.random.uniform(part_splits[2], (SLOTS, P_SIZE), jnp.float32) ** level_of(part_splits[2], (SLOTS, P_SIZE), ((0, 16),), -0.2, 0.2)), 0.3, 3.0),
        "occupied": jnp.clip(-2.0 + 1.6 * jax.random.uniform(part_splits[3], (SLOTS,), jnp.float32) ** level_of(part_splits[3], (SLOTS,), ((0, 16),), -0.2, 0.2), -2.0, -0.4),
        "coupling": centred(part_splits[4], (SLOTS, KMAX), 0.2, 3.0, ((0, 16),), jnp.float32),
        "degree": draw_degree(jax.random.fold_in(jax.random.fold_in(arg_keys[10], part), 71), part),
        "position": plant(jax.random.randint(part_splits[6], (SLOTS, KMAX), 0, N_PAIR * CAP), jax.random.fold_in(part_splits[6], 1), 0, (N_PAIR * CAP) - 1).astype(jnp.int32),
        "request": plant(jax.random.randint(part_splits[7], (N_PAIR, N_PAIR * CAP), 0, SLOTS_DEV), jax.random.fold_in(part_splits[7], 1), 0, SLOTS_DEV - 1).astype(jnp.int32),
        "pnos": centred(part_splits[8], (SLOTS, P_SIZE, DOM), 0.105, 1.5, ((0, 16),)),
        "domains": draw_domains(jax.random.fold_in(jax.random.fold_in(arg_keys[10], part), 71), part),
    }


def atom_columns(atom_slot, per_atom):
    offsets = jnp.arange(per_atom, dtype=jnp.int32)
    return (atom_slot[:, :, None] * per_atom + offsets[None, None, :]).reshape(atom_slot.shape[0], -1)


def intersection(own_pnos, own_atoms, other_pnos, other_atoms, per_atom):
    matches = own_atoms[:, :, None] == other_atoms[:, None, :]
    slot_ids = jnp.arange(own_atoms.shape[1], dtype=jnp.int32)
    position_in = jnp.sum(jnp.where(matches, slot_ids[None, None, :], 0), axis=2).astype(jnp.int32)
    present = jnp.any(matches, axis=2)
    columns = atom_columns(position_in, per_atom)
    kept_mask = jnp.repeat(present, per_atom, axis=1)
    picked = jnp.take_along_axis(other_pnos, jnp.broadcast_to(columns[:, None, :], other_pnos.shape), axis=2)
    mapped = jnp.where(kept_mask[:, None, :], picked, jnp.zeros_like(picked))
    return jnp.einsum("spy,sqy->spq", own_pnos.astype(jnp.float32), mapped.astype(jnp.float32))


def transform(intersection_mat, partner_block):
    left_half = jnp.einsum("spq,sqr->spr", intersection_mat, partner_block, precision=lax.Precision.HIGHEST)
    return jnp.einsum("spr,str->spt", left_half, intersection_mat, precision=lax.Precision.HIGHEST)


def reference(amplitudes, integrals, virtual, occupied, coupling, degree, position, request, pnos, domains):
    devices = SLOTS // SLOTS_DEV
    owner_dev = jnp.arange(SLOTS, dtype=jnp.int32) // SLOTS_DEV
    picked_ids = request[owner_dev[:, None], position]
    partner = ((position // CAP) * SLOTS_DEV + picked_ids).astype(jnp.int32)
    live_mask = jnp.arange(KMAX, dtype=jnp.int32)[None, :] < degree[:, None]
    weight = jnp.where(live_mask, coupling, jnp.zeros_like(coupling))
    denominator = (virtual[:, :, None] + virtual[:, None, :] - occupied[:, None, None]).reshape(SLOTS, P_SIZE * P_SIZE)

    def coupled_sum(current):
        def device_block(inputs):
            own_pnos, own_atoms, partner_ids, weight_rows = inputs
            flat_ids = partner_ids.reshape(-1)
            other_pnos = pnos[flat_ids]
            other_atoms = domains[flat_ids]
            other_amps = current[flat_ids].reshape(-1, P_SIZE, P_SIZE)
            repeated_pnos = jnp.repeat(own_pnos, KMAX, axis=0)
            repeated_atoms = jnp.repeat(own_atoms, KMAX, axis=0)
            intersection_mat = intersection(repeated_pnos, repeated_atoms, other_pnos, other_atoms, B)
            product = transform(intersection_mat, other_amps).reshape(SLOTS_DEV, KMAX, P_SIZE * P_SIZE)
            return jnp.sum(weight_rows[:, :, None] * product, axis=1)

        summed = lax.map(device_block, (pnos.reshape(devices, SLOTS_DEV, P_SIZE, DOM), domains.reshape(devices, SLOTS_DEV, NA), partner.reshape(devices, SLOTS_DEV, KMAX), weight.reshape(devices, SLOTS_DEV, KMAX)))
        return summed.reshape(SLOTS, P_SIZE * P_SIZE)

    current = amplitudes
    residual = jnp.zeros_like(amplitudes)
    for sweep in range(SWEEPS):
        coupled_term = coupled_sum(current)
        residual = integrals + denominator * current - coupled_term
        current = current - residual / denominator
    return current, residual
```

```python
import functools
import jax
import jax.numpy as jnp
from jax import lax
from jax.experimental import pallas as pl
from jax.experimental.pallas import tpu as pltpu
from jax.sharding import Mesh, PartitionSpec as P

ATOMS = 32
CHUNK = 8
VMEM_LIMIT = 48 * 1024 * 1024
NT = (((1,), (1,)), ((), ()))


def split(value):
    high = value.astype(jnp.bfloat16)
    low = (value - high.astype(jnp.float32)).astype(jnp.bfloat16)
    return high, low


def sweep_chunk(half_ref, weight_ref, amp_ref, cat_ref, left_ref, acc_ref):
    pairs, rows2, lanes = cat_ref.shape
    size = rows2 // 2
    chunk = pl.program_id(0)
    near = amp_ref.shape[0] // 2
    group = lax.broadcasted_iota(jnp.int32, (size, 4 * size), 1) // size
    even = (group % 2 == 0).astype(jnp.float32).astype(jnp.bfloat16)
    odd = (group % 2 == 1).astype(jnp.float32).astype(jnp.bfloat16)
    for j in range(lanes // (2 * size)):
        cols = slice(j * 2 * size, (j + 1) * 2 * size)
        entry = chunk * (lanes // (2 * size)) + j
        source = (entry % 2 + half_ref[0]) % 2 * near + entry // 2
        amp = amp_ref[source]
        first, second = amp * even, amp * odd
        right = jnp.concatenate([first, second, first, second], axis=0)
        high = cat_ref[:, :size, cols].reshape(pairs * size, 2 * size)
        low = cat_ref[:, size:, cols].reshape(pairs * size, 2 * size)
        both = jnp.dot(
            jnp.concatenate([high, low], axis=1), right, preferred_element_type=jnp.float32
        )
        left = (both[:, : 2 * size] + both[:, 2 * size :]).reshape(pairs, size, 2 * size)
        left = left * weight_ref[0, :, cols].reshape(pairs, 1, 2 * size)
        left_high, left_low = split(left)
        left_ref[:, :size, cols] = left_high
        left_ref[:, size:, cols] = left_low
    for s in range(pairs):
        part = lax.dot_general(
            left_ref[s], cat_ref[s], NT, preferred_element_type=jnp.float32
        )
        acc_ref[s] = jnp.where(chunk == 0, part, acc_ref[s] + part)


def coupled_of(acc):
    size = acc.shape[0] // 2
    rows = acc[:size] + acc[size:]
    return rows[:, :size] + rows[:, size:]


def first_kernel(
    half_ref, wanted_ref, own_ref, pnos_ref, ids_ref, weight_ref, amp_ref, current_ref,
    integrals_ref, denominator_ref, cat_ref, new_ref, send_ref, full_ref, left_ref, acc_ref,
    even_ref, odd_ref,
):
    pairs, size, unused = current_ref.shape
    columns = own_ref.shape[1]
    width = pnos_ref.shape[2]

    row_ids = lax.broadcasted_iota(jnp.int32, (columns, width), 0)
    for p in range(pnos_ref.shape[0]):
        table = (row_ids == ids_ref[p]).astype(jnp.float32).astype(jnp.bfloat16)
        full_ref[p * size : (p + 1) * size, :] = lax.dot_general(
            pnos_ref[p], table, NT, preferred_element_type=jnp.float32
        ).astype(jnp.bfloat16)
    cross = lax.dot_general(own_ref[...], full_ref[...], NT, preferred_element_type=jnp.float32)
    high, low = split(cross)
    cat_ref[0, :, :size, :] = high.reshape(pairs, size, -1)
    cat_ref[0, :, size:, :] = low.reshape(pairs, size, -1)
    sweep_chunk(half_ref, weight_ref, amp_ref, cat_ref.at[0], left_ref, acc_ref)

    @pl.when(pl.program_id(0) == pl.num_programs(0) - 1)
    def finish():
        blank = jnp.zeros((size, size), jnp.float32)
        for s in range(pairs):
            denominator = denominator_ref[s]
            residual = integrals_ref[s] + denominator * current_ref[s] - coupled_of(acc_ref[s])
            new = current_ref[s] - residual / denominator
            new_ref[s] = new
            high, low = split(new)
            high, low = high.astype(jnp.float32), low.astype(jnp.float32)
            even_ref[s] = jnp.concatenate([high, blank, low, blank], axis=1).astype(jnp.bfloat16)
            odd_ref[s] = jnp.concatenate([blank, high, blank, low], axis=1).astype(jnp.bfloat16)

        def pack(d, carry):
            send_ref[d] = even_ref[wanted_ref[2 * d]] + odd_ref[wanted_ref[2 * d + 1]]
            return carry

        lax.fori_loop(0, send_ref.shape[0], pack, 0)


def second_kernel(
    half_ref, cat_ref, weight_ref, amp_ref, current_ref, integrals_ref, denominator_ref,
    new_ref, residual_ref, left_ref, acc_ref, new_rows_ref, residual_rows_ref,
):
    pairs, size, unused = current_ref.shape

    sweep_chunk(half_ref, weight_ref, amp_ref, cat_ref.at[0], left_ref, acc_ref)

    @pl.when(pl.program_id(0) == pl.num_programs(0) - 1)
    def finish():
        for s in range(pairs):
            denominator = denominator_ref[s]
            residual = integrals_ref[s] + denominator * current_ref[s] - coupled_of(acc_ref[s])
            rows = slice(s * size, (s + 1) * size)
            residual_rows_ref[rows, :] = residual
            new_rows_ref[rows, :] = current_ref[s] - residual / denominator
        for rows_ref, out_ref in ((residual_rows_ref, residual_ref), (new_rows_ref, new_ref)):
            for a in range(0, size, 2):
                out_ref[:, a * size : (a + 2) * size] = jnp.concatenate(
                    [rows_ref[pl.ds(a + i, pairs, stride=size), :] for i in range(2)], axis=1
                )


def smem():
    return pl.BlockSpec(memory_space=pltpu.SMEM)


def whole(shape):
    return pl.BlockSpec(shape, lambda i: (0,) * len(shape))


def by_chunk(shape):
    return pl.BlockSpec(shape, lambda i: (i,) + (0,) * (len(shape) - 1))


def params():
    return pltpu.CompilerParams(
        dimension_semantics=("arbitrary",), vmem_limit_bytes=VMEM_LIMIT
    )


def first_sweep(half, wanted, own, pnos, ids, weight, amp, current, integrals, denominator):
    pairs, size, unused = current.shape
    slots, unused, width = pnos.shape
    steps = slots // CHUNK
    sources = amp.shape[0]
    lanes = CHUNK * size
    block = (pairs, size, size)
    return pl.pallas_call(
        first_kernel,
        grid=(steps,),
        in_specs=[
            smem(), smem(), whole(own.shape), by_chunk((CHUNK, size, width)),
            by_chunk((CHUNK, 1, width)), by_chunk((1, pairs, lanes)), whole(amp.shape),
            whole(block), whole(block), whole(block),
        ],
        out_specs=[
            by_chunk((1, pairs, 2 * size, lanes)), whole(block), whole(amp.shape),
        ],
        out_shape=[
            jax.ShapeDtypeStruct((steps, pairs, 2 * size, lanes), jnp.bfloat16),
            jax.ShapeDtypeStruct(block, jnp.float32),
            jax.ShapeDtypeStruct(amp.shape, jnp.bfloat16),
        ],
        scratch_shapes=[
            pltpu.VMEM((lanes, own.shape[1]), jnp.bfloat16),
            pltpu.VMEM((pairs, 2 * size, lanes), jnp.bfloat16),
            pltpu.VMEM((pairs, 2 * size, 2 * size), jnp.float32),
            pltpu.VMEM((pairs, size, 4 * size), jnp.bfloat16),
            pltpu.VMEM((pairs, size, 4 * size), jnp.bfloat16),
        ],
        compiler_params=params(),
        name="first_sweep",
    )(half, wanted, own, pnos, ids, weight, amp, current, integrals, denominator)


def second_sweep(half, cat, weight, amp, current, integrals, denominator):
    pairs, size, unused = current.shape
    steps, lanes = cat.shape[0], cat.shape[3]
    block = (pairs, size, size)
    flat = (pairs, size * size)
    return pl.pallas_call(
        second_kernel,
        grid=(steps,),
        in_specs=[
            smem(), by_chunk((1,) + cat.shape[1:]), by_chunk((1, pairs, lanes)),
            whole(amp.shape), whole(block), whole(block), whole(block),
        ],
        out_specs=[whole(flat), whole(flat)],
        out_shape=[jax.ShapeDtypeStruct(flat, jnp.float32)] * 2,
        scratch_shapes=[
            pltpu.VMEM((pairs, 2 * size, lanes), jnp.bfloat16),
            pltpu.VMEM((pairs, 2 * size, 2 * size), jnp.float32),
            pltpu.VMEM((pairs * size, size), jnp.float32),
            pltpu.VMEM((pairs * size, size), jnp.float32),
        ],
        compiler_params=params(),
        name="second_sweep",
    )(half, cat, weight, amp, current, integrals, denominator)


def orbital_ids(atoms, per_atom):
    offsets = jnp.arange(per_atom, dtype=jnp.int32)
    return (atoms[:, :, None] * per_atom + offsets[None, None, :]).reshape(atoms.shape[0], -1)


def on_device(
    amplitudes, integrals, virtual, occupied, coupling, degree, position, request, pnos, domains
):
    pairs = amplitudes.shape[0]
    size = virtual.shape[1]
    depth = coupling.shape[1]
    per_atom = pnos.shape[2] // domains.shape[1]
    columns = ATOMS * per_atom
    slots = request.shape[1]
    sources = slots // 2
    near = sources // 2
    half = lax.axis_index("half").astype(jnp.int32)
    swap = [(0, 1), (1, 0)]
    block = (pairs, size, size)

    far_pnos = lax.ppermute(pnos, "half", swap)
    asked = request.reshape(2, near, 2).transpose(1, 0, 2)
    asked = lax.all_to_all(asked, "near", split_axis=0, concat_axis=0, tiled=True)
    here = lax.dynamic_index_in_dim(asked, half, 1, keepdims=False)
    there = lax.dynamic_index_in_dim(asked, 1 - half, 1, keepdims=False)
    from_far = lax.ppermute(there, "half", swap)
    wanted = jnp.where(
        half == 0, jnp.concatenate([here, from_far]), jnp.concatenate([from_far, here])
    ).reshape(-1)

    outgoing = jnp.stack([pnos[here], far_pnos[there]], axis=1)
    partner_pnos = lax.all_to_all(
        outgoing, "near", split_axis=0, concat_axis=0, tiled=True
    ).reshape(slots, size, -1)

    current = amplitudes.reshape(block)
    high = lax.reduce_precision(current, 8, 7)
    parts = jnp.stack([high, current - high], axis=0).astype(jnp.bfloat16)
    amp = parts[:, wanted].reshape(2, sources, 2, size, size)
    amp = amp.transpose(1, 3, 0, 2, 4).reshape(sources, size, 4 * size)
    amp = lax.all_to_all(amp, ("half", "near"), split_axis=0, concat_axis=0, tiled=True)

    all_domains = lax.all_gather(domains, ("half", "near"), tiled=True)
    slot = jnp.arange(slots, dtype=jnp.int32)
    slot_source = (slot // 2 % 2 + half) % 2 * near + slot // 4
    slot_entry = slot_source * 2 + slot % 2
    partner = slot_source * pairs + request[0, slot_entry]
    ids = orbital_ids(all_domains[partner], per_atom)[:, None, :]
    live = jnp.arange(depth, dtype=jnp.int32)[None, :] < degree[:, None]
    weight = jnp.where(live, coupling, jnp.zeros_like(coupling))
    hit = position[:, :, None] == slot_entry[None, None, :]
    slot_weight = jnp.sum(jnp.where(hit, weight[:, :, None], 0.0), axis=1)
    slot_weight = jnp.repeat(slot_weight, size, axis=1)
    slot_weight = slot_weight.reshape(pairs, slots // CHUNK, CHUNK * size).transpose(1, 0, 2)

    own_ids = orbital_ids(domains, per_atom)
    table = own_ids[:, :, None] == jnp.arange(columns, dtype=jnp.int32)[None, None, :]
    own = jnp.einsum(
        "sqz,szy->sqy", pnos, table.astype(jnp.bfloat16), preferred_element_type=jnp.float32
    ).astype(jnp.bfloat16).reshape(pairs * size, columns)

    denominator = virtual[:, :, None] + virtual[:, None, :] - occupied[:, None, None]
    integrals = integrals.reshape(block)
    half = half.reshape(1)
    cat, current, amp = first_sweep(
        half, wanted, own, partner_pnos, ids, slot_weight, amp, current, integrals, denominator
    )
    amp = lax.all_to_all(amp, ("half", "near"), split_axis=0, concat_axis=0, tiled=True)
    new, residual = second_sweep(
        half, cat, slot_weight, amp, current, integrals, denominator
    )
    return new, residual


def solution(mesh):
    count = mesh.shape["pair"]
    devices = mesh.devices.reshape(mesh.shape["frag"], 2, count // 2)
    split_mesh = Mesh(devices, ("frag", "half", "near"))
    rows = ("frag", "half", "near")
    return jax.shard_map(
        on_device,
        mesh=split_mesh,
        in_specs=(
            P(rows, None), P(rows, None), P(rows, None), P(rows), P(rows, None),
            P(rows), P(rows, None), P(rows, None), P(rows, None, None), P(rows, None),
        ),
        out_specs=(P(rows, None), P(rows, None)),
        check_vma=False,
    )
```

```python
import functools
import jax
import jax.numpy as jnp
from jax import lax
from jax.experimental import pallas as pl
from jax.experimental.pallas import tpu as pltpu
from jax.sharding import Mesh, PartitionSpec as P

ATOMS = 32
NEAR_STEP = 4
ATOM_ROWS = 16
VMEM_LIMIT = 48 * 1024 * 1024
NT = (((1,), (1,)), ((), ()))


def split(value):
    high = value.astype(jnp.bfloat16)
    low = (value - high.astype(jnp.float32)).astype(jnp.bfloat16)
    return high, low


def store_parts(value, even_ref, odd_ref, p):
    high, low = split(value)
    high, low = high.astype(jnp.float32), low.astype(jnp.float32)
    blank = jnp.zeros_like(high)
    even_ref[p] = jnp.concatenate([high, blank, low, blank], axis=1).astype(jnp.bfloat16)
    odd_ref[p] = jnp.concatenate([blank, high, blank, low], axis=1).astype(jnp.bfloat16)


def pack_kernel(
    column_ref, request_ref, pnos_ref, amp_ref, atoms_ref, out_ref, rows_ref, even_ref, odd_ref
):
    pairs, size, width = pnos_ref.shape
    for a in range(0, size, 2):
        both = amp_ref[:, a * size : (a + 2) * size]
        rows_ref[pl.ds(a, pairs, stride=size), :] = both[:, :size]
        rows_ref[pl.ds(a + 1, pairs, stride=size), :] = both[:, size:]
    for p in range(pairs):
        store_parts(rows_ref[p * size : (p + 1) * size, :], even_ref, odd_ref, p)
    first_row = lax.broadcasted_iota(jnp.int32, (ATOM_ROWS, width), 0) == 0

    def pack(n, carry):
        first = request_ref[n, 0, column_ref[0]]
        second = request_ref[n, 0, column_ref[0] + 1]
        out_ref[n, :size] = pnos_ref[first]
        out_ref[n, size : 2 * size] = pnos_ref[second]
        out_ref[n, 2 * size : 3 * size] = even_ref[first] + odd_ref[second]
        out_ref[n, 3 * size :] = jnp.where(
            first_row, atoms_ref[pl.ds(first, 1), :], atoms_ref[pl.ds(second, 1), :]
        ).astype(jnp.bfloat16)
        return carry

    lax.fori_loop(0, out_ref.shape[0], pack, 0)


def slot_weights(base, weight_ref, position_ref, slots, size):
    lane = lax.broadcasted_iota(jnp.int32, (1, slots * size), 1) // size + base
    total = jnp.zeros((weight_ref.shape[0], slots * size), jnp.float32)
    for c in range(weight_ref.shape[1]):
        hit = position_ref[:, c : c + 1] == lane
        total += jnp.where(hit, weight_ref[:, c : c + 1], 0.0)
    return total


def sweep_chunk(weights, amps, cat_ref, left_ref, acc_ref, before):
    pairs, rows2, lanes = cat_ref.shape
    size = rows2 // 2
    group = lax.broadcasted_iota(jnp.int32, (size, 4 * size), 1) // size
    even = (group % 2 == 0).astype(jnp.float32).astype(jnp.bfloat16)
    odd = (group % 2 == 1).astype(jnp.float32).astype(jnp.bfloat16)
    for j in range(lanes // (2 * size)):
        cols = slice(j * 2 * size, (j + 1) * 2 * size)
        amp = amps(j)
        first, second = amp * even, amp * odd
        right = jnp.concatenate([first, second, first, second], axis=0)
        high = cat_ref[:, :size, cols].reshape(pairs * size, 2 * size)
        low = cat_ref[:, size:, cols].reshape(pairs * size, 2 * size)
        both = jnp.dot(
            jnp.concatenate([high, low], axis=1), right, preferred_element_type=jnp.float32
        )
        left = (both[:, : 2 * size] + both[:, 2 * size :]).reshape(pairs, size, 2 * size)
        left = left * weights[:, cols].reshape(pairs, 1, 2 * size)
        left_high, left_low = split(left)
        left_ref[:, :size, cols] = left_high
        left_ref[:, size:, cols] = left_low
    for s in range(pairs):
        part = lax.dot_general(left_ref[s], cat_ref[s], NT, preferred_element_type=jnp.float32)
        acc_ref[s] = before(s) + part


def cross_chunk(own_ref, payload_ref, cat_ref, full_ref):
    columns = own_ref.shape[1]
    pairs, rows2, unused = cat_ref.shape
    size = rows2 // 2
    width = payload_ref.shape[2]
    row = lax.broadcasted_iota(jnp.int32, (columns, width), 0)
    column = lax.broadcasted_iota(jnp.int32, (1, width), 1)
    per_atom = columns // ATOMS
    for n in range(payload_ref.shape[0]):
        atoms = payload_ref[n, 3 * size :, :].astype(jnp.float32).astype(jnp.int32)
        for c in range(2):
            ids = atoms[c : c + 1, :] * per_atom + column % per_atom
            table = (row == ids).astype(jnp.float32).astype(jnp.bfloat16)
            start = (2 * n + c) * size
            full_ref[start : start + size, :] = lax.dot_general(
                payload_ref[n, c * size : (c + 1) * size, :], table, NT,
                preferred_element_type=jnp.float32,
            ).astype(jnp.bfloat16)
    cross = lax.dot_general(own_ref[...], full_ref[...], NT, preferred_element_type=jnp.float32)
    high, low = split(cross)
    cat_ref[:, :size, :] = high.reshape(pairs, size, -1)
    cat_ref[:, size:, :] = low.reshape(pairs, size, -1)


def coupled_of(acc):
    size = acc.shape[0] // 2
    rows = acc[:size] + acc[size:]
    return rows[:, :size] + rows[:, size:]


def near_chunk(base, own_ref, payload_ref, weight_ref, position_ref, cat_ref, full_ref, left_ref,
               acc_ref, before):
    size = cat_ref.shape[1] // 2
    slots = 2 * payload_ref.shape[0]
    cross_chunk(own_ref, payload_ref, cat_ref, full_ref)
    weights = slot_weights(
        base + pl.program_id(0) * slots, weight_ref, position_ref, slots, size
    )
    sweep_chunk(
        weights, lambda j: payload_ref[j, 2 * size : 3 * size, :], cat_ref, left_ref, acc_ref,
        before,
    )


def first_kernel(
    base_ref, own_ref, payload_ref, weight_ref, position_ref, cat_ref, out_ref, full_ref,
    left_ref, acc_ref,
):
    first = pl.program_id(0) == 0
    near_chunk(
        base_ref[0], own_ref, payload_ref, weight_ref, position_ref, cat_ref.at[0], full_ref,
        left_ref, acc_ref, lambda s: jnp.where(first, 0.0, acc_ref[s]),
    )

    @pl.when(pl.program_id(0) == pl.num_programs(0) - 1)
    def finish():
        out_ref[...] = acc_ref[...]


def first_end_kernel(
    base_ref, here_ref, there_ref, own_ref, payload_ref, weight_ref, position_ref, before_ref,
    current_ref, integrals_ref, denominator_ref, cat_ref, new_ref, send_ref, full_ref, left_ref,
    acc_ref, even_ref, odd_ref,
):
    pairs, size, unused = current_ref.shape
    near = here_ref.shape[0]
    first = pl.program_id(0) == 0
    near_chunk(
        base_ref[0], own_ref, payload_ref, weight_ref, position_ref, cat_ref.at[0], full_ref,
        left_ref, acc_ref, lambda s: jnp.where(first, before_ref[s], acc_ref[s]),
    )

    @pl.when(pl.program_id(0) == pl.num_programs(0) - 1)
    def finish():
        for s in range(pairs):
            denominator = denominator_ref[s]
            residual = integrals_ref[s] + denominator * current_ref[s] - coupled_of(acc_ref[s])
            new = current_ref[s] - residual / denominator
            new_ref[s] = new
            store_parts(new, even_ref, odd_ref, s)

        far_start = base_ref[0] // 2
        near_start = near - far_start
        column = base_ref[1]

        def pack(n, carry):
            for start, table_ref in ((near_start, here_ref), (far_start, there_ref)):
                first = table_ref[n, 0, column]
                second = table_ref[n, 0, column + 1]
                send_ref[start + n] = even_ref[first] + odd_ref[second]
            return carry

        lax.fori_loop(0, near, pack, 0)


def second_kernel(
    base_ref, near_cat_ref, far_cat_ref, weight_ref, position_ref, near_amp_ref, far_amp_ref,
    current_ref, integrals_ref, denominator_ref, new_ref, residual_ref, left_ref, acc_ref,
    new_rows_ref, residual_rows_ref,
):
    pairs, size, unused = current_ref.shape
    step = pl.program_id(0)
    slots = near_cat_ref.shape[3] // size
    first = step == 0
    parts = ((0, near_cat_ref, near_amp_ref), (1, far_cat_ref, far_amp_ref))
    for part, cat_ref, amp_ref in parts:
        weights = slot_weights(
            base_ref[part] + step * slots, weight_ref, position_ref, slots, size
        )
        if part == 0:
            before = lambda s: jnp.where(first, 0.0, acc_ref[s])
        else:
            before = lambda s: acc_ref[s]
        sweep_chunk(
            weights, lambda j: amp_ref[j], cat_ref.at[0], left_ref.at[part], acc_ref, before
        )

    @pl.when(step == pl.num_programs(0) - 1)
    def finish():
        for s in range(pairs):
            denominator = denominator_ref[s]
            residual = integrals_ref[s] + denominator * current_ref[s] - coupled_of(acc_ref[s])
            rows = slice(s * size, (s + 1) * size)
            residual_rows_ref[rows, :] = residual
            new_rows_ref[rows, :] = current_ref[s] - residual / denominator
        for rows_ref, out_ref in ((residual_rows_ref, residual_ref), (new_rows_ref, new_ref)):
            for a in range(0, size, 2):
                out_ref[:, a * size : (a + 2) * size] = jnp.concatenate(
                    [rows_ref[pl.ds(a + i, pairs, stride=size), :] for i in range(2)], axis=1
                )


def smem():
    return pl.BlockSpec(memory_space=pltpu.SMEM)


def whole(shape):
    return pl.BlockSpec(shape, lambda i, *refs: (0,) * len(shape))


def by_step(shape):
    return pl.BlockSpec(shape, lambda i, *refs: (i,) + (0,) * (len(shape) - 1))


def params():
    return pltpu.CompilerParams(
        dimension_semantics=("arbitrary",), vmem_limit_bytes=VMEM_LIMIT
    )


def pack_payload(column, requests, pnos, amplitudes, atoms):
    pairs, size, width = pnos.shape
    near = requests.shape[0]
    return pl.pallas_call(
        pack_kernel,
        in_specs=[smem(), smem()] + [pl.BlockSpec(memory_space=pltpu.VMEM)] * 3,
        out_specs=pl.BlockSpec(memory_space=pltpu.VMEM),
        out_shape=jax.ShapeDtypeStruct((near, 3 * size + ATOM_ROWS, width), jnp.bfloat16),
        scratch_shapes=[
            pltpu.VMEM((pairs * size, size), jnp.float32),
            pltpu.VMEM((pairs, size, 4 * size), jnp.bfloat16),
            pltpu.VMEM((pairs, size, 4 * size), jnp.bfloat16),
        ],
        compiler_params=pltpu.CompilerParams(vmem_limit_bytes=VMEM_LIMIT),
        name="pack_payload",
    )(column, requests, pnos, amplitudes, atoms)


def chunk_shapes(own, payload, pairs, size):
    near, rows, width = payload.shape
    lanes = 2 * NEAR_STEP * size
    cat = (near // NEAR_STEP, pairs, 2 * size, lanes)
    scratch = [
        pltpu.VMEM((lanes, own.shape[1]), jnp.bfloat16),
        pltpu.VMEM((pairs, 2 * size, lanes), jnp.bfloat16),
        pltpu.VMEM((pairs, 2 * size, 2 * size), jnp.float32),
    ]
    return cat, (NEAR_STEP, rows, width), (pairs, 2 * size, 2 * size), scratch


def first_sweep(base, own, payload, weight, position, size):
    pairs = weight.shape[0]
    cat, chunk, acc, scratch = chunk_shapes(own, payload, pairs, size)
    return pl.pallas_call(
        first_kernel,
        grid=(cat[0],),
        in_specs=[
            smem(), whole(own.shape), by_step(chunk), whole(weight.shape), whole(position.shape)
        ],
        out_specs=[by_step((1,) + cat[1:]), whole(acc)],
        out_shape=[
            jax.ShapeDtypeStruct(cat, jnp.bfloat16), jax.ShapeDtypeStruct(acc, jnp.float32)
        ],
        scratch_shapes=scratch,
        compiler_params=params(),
        name="first_sweep_near",
    )(base, own, payload, weight, position)


def first_sweep_end(
    base, here, there, own, payload, weight, position, before, current, integrals, denominator
):
    pairs, size, unused = current.shape
    cat, chunk, acc, scratch = chunk_shapes(own, payload, pairs, size)
    block = (pairs, size, size)
    parts = (pairs, size, 4 * size)
    send = (2 * here.shape[0],) + parts[1:]
    return pl.pallas_call(
        first_end_kernel,
        grid=(cat[0],),
        in_specs=[
            smem(), smem(), smem(), whole(own.shape), by_step(chunk), whole(weight.shape),
            whole(position.shape), whole(acc), whole(block), whole(block), whole(block),
        ],
        out_specs=[by_step((1,) + cat[1:]), whole(block), whole(send)],
        out_shape=[
            jax.ShapeDtypeStruct(cat, jnp.bfloat16),
            jax.ShapeDtypeStruct(block, jnp.float32),
            jax.ShapeDtypeStruct(send, jnp.bfloat16),
        ],
        scratch_shapes=scratch + [pltpu.VMEM(parts, jnp.bfloat16)] * 2,
        compiler_params=params(),
        name="first_sweep_far",
    )(base, here, there, own, payload, weight, position, before, current, integrals, denominator)


def second_sweep(
    base, near_cat, far_cat, weight, position, amp, current, integrals, denominator
):
    pairs, size, unused = current.shape
    steps, lanes = near_cat.shape[0], near_cat.shape[3]
    block = (pairs, size, size)
    flat = (pairs, size * size)
    cat = by_step((1,) + near_cat.shape[1:])
    amp_block = (NEAR_STEP,) + amp.shape[1:]
    grid_spec = pltpu.PrefetchScalarGridSpec(
        num_scalar_prefetch=1,
        grid=(steps,),
        in_specs=[
            cat, cat, whole(weight.shape), whole(position.shape),
            pl.BlockSpec(
                amp_block, lambda i, base: (base[0] // (2 * NEAR_STEP) + i, 0, 0)
            ),
            pl.BlockSpec(
                amp_block, lambda i, base: (base[1] // (2 * NEAR_STEP) + i, 0, 0)
            ),
            whole(block), whole(block), whole(block),
        ],
        out_specs=[whole(flat), whole(flat)],
        scratch_shapes=[
            pltpu.VMEM((2, pairs, 2 * size, lanes), jnp.bfloat16),
            pltpu.VMEM((pairs, 2 * size, 2 * size), jnp.float32),
            pltpu.VMEM((pairs * size, size), jnp.float32),
            pltpu.VMEM((pairs * size, size), jnp.float32),
        ],
    )
    return pl.pallas_call(
        second_kernel,
        grid_spec=grid_spec,
        out_shape=[jax.ShapeDtypeStruct(flat, jnp.float32)] * 2,
        compiler_params=params(),
        name="second_sweep",
    )(base, near_cat, far_cat, weight, position, amp, amp, current, integrals, denominator)


def on_device(
    amplitudes, integrals, virtual, occupied, coupling, degree, position, request, pnos, domains
):
    pairs = amplitudes.shape[0]
    size = virtual.shape[1]
    depth = coupling.shape[1]
    width = pnos.shape[2]
    per_atom = width // domains.shape[1]
    columns = ATOMS * per_atom
    slots = request.shape[1]
    near = slots // 4
    half = lax.axis_index("half").astype(jnp.int32)
    mine = lax.axis_index("near").astype(jnp.int32)
    swap = [(0, 1), (1, 0)]
    block = (pairs, size, size)

    far_pnos = lax.ppermute(pnos, "half", swap)
    far_amplitudes = lax.ppermute(amplitudes, "half", swap)
    atoms = jnp.repeat(domains, per_atom, axis=1)
    far_domains = lax.ppermute(domains, "half", swap)
    far_atoms = jnp.repeat(far_domains, per_atom, axis=1)
    here = jnp.broadcast_to(request[None], (near, 1, slots))
    here = lax.all_to_all(here, "near", split_axis=0, concat_axis=0, tiled=True)
    there = lax.ppermute(here, "half", swap)

    near_base = half * 2 * near
    far_base = (1 - half) * 2 * near
    near_column = near_base + 2 * mine
    far_column = far_base + 2 * mine
    outgoing = pack_payload(near_column.reshape(1), here, pnos, amplitudes, atoms.astype(jnp.float32))
    near_payload = lax.all_to_all(outgoing, "near", split_axis=0, concat_axis=0, tiled=True)
    outgoing = pack_payload(
        far_column.reshape(1), here, far_pnos, far_amplitudes, far_atoms.astype(jnp.float32)
    )
    far_payload = lax.all_to_all(outgoing, "near", split_axis=0, concat_axis=0, tiled=True)

    live = jnp.arange(depth, dtype=jnp.int32)[None, :] < degree[:, None]
    weight = jnp.where(live, coupling, jnp.zeros_like(coupling))

    own_ids = atoms * per_atom + jnp.arange(width, dtype=jnp.int32)[None, :] % per_atom
    table = own_ids[:, :, None] == jnp.arange(columns, dtype=jnp.int32)[None, None, :]
    own = jnp.einsum(
        "sqz,szy->sqy", pnos, table.astype(jnp.bfloat16), preferred_element_type=jnp.float32
    ).astype(jnp.bfloat16).reshape(pairs * size, columns)

    denominator = virtual[:, :, None] + virtual[:, None, :] - occupied[:, None, None]
    current = amplitudes.reshape(block)
    integrals = integrals.reshape(block)
    near_cat, before = first_sweep(
        near_base.reshape(1), own, near_payload, weight, position, size
    )
    far_cat, current, amp = first_sweep_end(
        jnp.stack([far_base, near_column]), here, there, own, far_payload, weight, position,
        before, current, integrals, denominator,
    )
    amp = lax.all_to_all(amp, ("half", "near"), split_axis=0, concat_axis=0, tiled=True)
    new, residual = second_sweep(
        jnp.stack([near_base, far_base]), near_cat, far_cat, weight, position, amp, current,
        integrals, denominator,
    )
    return new, residual


def solution(mesh):
    count = mesh.shape["pair"]
    devices = mesh.devices.reshape(mesh.shape["frag"], 2, count // 2)
    split_mesh = Mesh(devices, ("frag", "half", "near"))
    rows = ("frag", "half", "near")
    return jax.shard_map(
        on_device,
        mesh=split_mesh,
        in_specs=(
            P(rows, None), P(rows, None), P(rows, None), P(rows), P(rows, None),
            P(rows), P(rows, None), P(rows, None), P(rows, None, None), P(rows, None),
        ),
        out_specs=(P(rows, None), P(rows, None)),
        check_vma=False,
    )
```

```python
import functools
import jax
import jax.numpy as jnp
from jax import lax
from jax.experimental import pallas as pl
from jax.experimental.pallas import tpu as pltpu
from jax.sharding import Mesh, PartitionSpec as P

ATOMS = 32
ONE_STEP = 8
NEAR_STEP = 4
CUTS = 4
CODE_TOP = 32767.0
CODE_ROWS = 16
SMALLEST = 2.0**-100
VMEM_LIMIT = 24 * 1024 * 1024
NT = (((1,), (1,)), ((), ()))


def split(value):
    high = value.astype(jnp.bfloat16)
    low = (value - high.astype(jnp.float32)).astype(jnp.bfloat16)
    return high, low


def store_parts(value, even_ref, odd_ref, p):
    high, low = split(value)
    high, low = high.astype(jnp.float32), low.astype(jnp.float32)
    blank = jnp.zeros_like(high)
    even_ref[p] = jnp.concatenate([high, blank, low, blank], axis=1).astype(jnp.bfloat16)
    odd_ref[p] = jnp.concatenate([blank, high, blank, low], axis=1).astype(jnp.bfloat16)


def store_codes(value, even_ref, odd_ref, p):
    size = value.shape[0]
    top = jnp.maximum(jnp.max(jnp.abs(value), axis=0, keepdims=True), SMALLEST)
    eighths = jnp.ceil(jnp.log2(top) * 8.0)
    codes = jnp.clip(jnp.round(value * (CODE_TOP / scale_of(eighths))), -CODE_TOP, CODE_TOP)
    rows = jnp.concatenate([codes, jnp.broadcast_to(eighths, (CODE_ROWS, size))], axis=0)
    blank = jnp.zeros_like(rows)
    for ref, parts in ((even_ref, [rows, blank]), (odd_ref, [blank, rows])):
        ref[p] = jnp.concatenate(parts, axis=1).astype(jnp.int32).astype(jnp.int16)


def scale_of(eighths):
    return jnp.exp2(eighths * 0.125)


def parts_of_codes(codes):
    rows = codes.astype(jnp.int32).astype(jnp.float32)
    size = rows.shape[0] - CODE_ROWS
    scale = scale_of(rows[size : size + 1, :]) * (1.0 / CODE_TOP)
    return jnp.concatenate(split(rows[:size, :] * scale), axis=1)


def to_blocks(flat_ref, rows_ref, size):
    pairs = flat_ref.shape[0]
    for a in range(0, size, 2):
        both = flat_ref[:, a * size : (a + 2) * size]
        rows_ref[pl.ds(a, pairs, stride=size), :] = both[:, :size]
        rows_ref[pl.ds(a + 1, pairs, stride=size), :] = both[:, size:]


def atoms_of_columns(domains, width):
    count = domains.shape[1]
    entry = lax.broadcasted_iota(jnp.int32, (count, width), 0)
    column = lax.broadcasted_iota(jnp.int32, (count, width), 1)
    spread = (entry == column // (width // count)).astype(jnp.float32).astype(jnp.bfloat16)
    atoms = domains.astype(jnp.float32).astype(jnp.bfloat16)
    return jnp.dot(atoms, spread, preferred_element_type=jnp.float32)


def column_table(atoms, columns):
    width = atoms.shape[1]
    per_atom = columns // ATOMS
    row = lax.broadcasted_iota(jnp.int32, (columns, width), 0)
    column = lax.broadcasted_iota(jnp.int32, (1, width), 1)
    ids = atoms.astype(jnp.int32) * per_atom + column % per_atom
    return (row == ids).astype(jnp.float32).astype(jnp.bfloat16)


def prepare_kernel(
    pnos_ref, domains_ref, amp_ref, integrals_ref, own_ref, current_ref, blocks_ref, atoms_ref
):
    pairs, size, width = pnos_ref.shape
    columns = own_ref.shape[1]
    to_blocks(amp_ref, current_ref, size)
    to_blocks(integrals_ref, blocks_ref, size)
    atoms_ref[...] = atoms_of_columns(domains_ref[...], width)
    for p in range(pairs):
        own_ref[p * size : (p + 1) * size, :] = lax.dot_general(
            pnos_ref[p], column_table(atoms_ref[p : p + 1, :], columns), NT,
            preferred_element_type=jnp.float32,
        ).astype(jnp.bfloat16)


def pack_kernel(
    column_ref, table_ref, pnos_ref, amp_ref, out_ref, rows_ref, even_ref, odd_ref
):
    pairs, size, unused = pnos_ref.shape
    to_blocks(amp_ref, rows_ref, size)
    for p in range(pairs):
        store_parts(rows_ref[p * size : (p + 1) * size, :], even_ref, odd_ref, p)

    def pack(n, carry):
        first = table_ref[n, 0, column_ref[0]]
        second = table_ref[n, 0, column_ref[0] + 1]
        out_ref[n, :size] = pnos_ref[first]
        out_ref[n, size : 2 * size] = pnos_ref[second]
        out_ref[n, 2 * size :] = even_ref[first] + odd_ref[second]
        return carry

    lax.fori_loop(0, out_ref.shape[0], pack, 0)


def slot_weights(base, weight_ref, position_ref, slots, size):
    lane = lax.broadcasted_iota(jnp.int32, (1, slots * size), 1) // size + base
    total = jnp.zeros((weight_ref.shape[0], slots * size), jnp.float32)
    for c in range(weight_ref.shape[1]):
        hit = position_ref[:, c : c + 1] == lane
        total += jnp.where(hit, weight_ref[:, c : c + 1], 0.0)
    return total


def sweep_chunk(weights, amps, cat_ref, left_ref, acc_ref, before, ready=lambda j: None):
    pairs, rows2, lanes = cat_ref.shape
    size = rows2 // 2
    group = lax.broadcasted_iota(jnp.int32, (size, 4 * size), 1) // size
    even = (group % 2 == 0).astype(jnp.float32).astype(jnp.bfloat16)
    odd = (group % 2 == 1).astype(jnp.float32).astype(jnp.bfloat16)
    for j in range(lanes // (2 * size)):
        cols = slice(j * 2 * size, (j + 1) * 2 * size)
        ready(j)
        amp = amps(j)
        first, second = amp * even, amp * odd
        right = jnp.concatenate([first, second, first, second], axis=0)
        high = cat_ref[:, :size, cols].reshape(pairs * size, 2 * size)
        low = cat_ref[:, size:, cols].reshape(pairs * size, 2 * size)
        both = jnp.dot(
            jnp.concatenate([high, low], axis=1), right, preferred_element_type=jnp.float32
        )
        left = (both[:, : 2 * size] + both[:, 2 * size :]).reshape(pairs, size, 2 * size)
        left = left * weights[:, cols].reshape(pairs, 1, 2 * size)
        left_high, left_low = split(left)
        left_ref[:, :size, cols] = left_high
        left_ref[:, size:, cols] = left_low
    for s in range(pairs):
        part = lax.dot_general(left_ref[s], cat_ref[s], NT, preferred_element_type=jnp.float32)
        acc_ref[s] = before(s) + part


def cross_chunk(slot_atoms, own_ready, own_ref, payload_ref, cat_ref, full_ref):
    columns = own_ref.shape[1]
    pairs, rows2, unused = cat_ref.shape
    size = rows2 // 2
    for k in range(2 * payload_ref.shape[0]):
        n, c = k // 2, k % 2
        full_ref[k * size : (k + 1) * size, :] = lax.dot_general(
            payload_ref[n, c * size : (c + 1) * size, :], column_table(slot_atoms(k), columns),
            NT, preferred_element_type=jnp.float32,
        ).astype(jnp.bfloat16)
    own_ready()
    cross = lax.dot_general(own_ref[...], full_ref[...], NT, preferred_element_type=jnp.float32)
    high, low = split(cross)
    cat_ref[:, :size, :] = high.reshape(pairs, size, -1)
    cat_ref[:, size:, :] = low.reshape(pairs, size, -1)


def coupled_of(acc):
    size = acc.shape[0] // 2
    rows = acc[:size] + acc[size:]
    return rows[:, :size] + rows[:, size:]


def near_chunk(
    base, request_ref, table_ref, own_hbm, payload_ref, weight_ref, position_ref, cat_hbm,
    own_ref, cat_ref, full_ref, left_ref, acc_ref, sem_ref,
):
    size = cat_ref.shape[1] // 2
    width = payload_ref.shape[2]
    pairs = weight_ref.shape[0]
    slots = 2 * payload_ref.shape[0]
    step = pl.program_id(0)
    entries = (table_ref.shape[2] - request_ref.shape[1]) // pairs
    own_copy = pltpu.make_async_copy(own_hbm, own_ref, sem_ref.at[0])

    @pl.when(step == 0)
    def fetch():
        own_copy.start()

    def own_ready():
        @pl.when(step == 0)
        def wait():
            own_copy.wait()

    entry = lax.broadcasted_iota(jnp.int32, (1, width), 1) // (width // entries)

    def slot_atoms(k):
        slot = step * slots + k
        start = request_ref.shape[1] + request_ref[0, base + slot] * entries
        atoms = jnp.zeros((1, width), jnp.int32)
        for a in range(entries):
            atoms = jnp.where(entry == a, table_ref[slot // 2, 0, start + a], atoms)
        return atoms

    cross_chunk(slot_atoms, own_ready, own_ref, payload_ref, cat_ref, full_ref)
    cat_copy = pltpu.make_async_copy(cat_ref, cat_hbm.at[step], sem_ref.at[1])
    cat_copy.start()
    weights = slot_weights(base + step * slots, weight_ref, position_ref, slots, size)
    sweep_chunk(
        weights, lambda j: payload_ref[j, 2 * size :, :], cat_ref, left_ref, acc_ref,
        lambda s: jnp.where(step == 0, 0.0, acc_ref[s]),
    )
    cat_copy.wait()


def first_kernel(
    base_ref, request_ref, table_ref, own_hbm, payload_ref, weight_ref, position_ref, cat_hbm,
    acc_hbm, own_ref, cat_ref, full_ref, left_ref, acc_ref, sem_ref,
):
    near_chunk(
        base_ref[0], request_ref, table_ref, own_hbm, payload_ref, weight_ref, position_ref,
        cat_hbm, own_ref, cat_ref, full_ref, left_ref, acc_ref, sem_ref,
    )

    @pl.when(pl.program_id(0) == pl.num_programs(0) - 1)
    def finish():
        copy = pltpu.make_async_copy(acc_ref, acc_hbm, sem_ref.at[2])
        copy.start()
        copy.wait()


def first_end_kernel(
    base_ref, request_ref, here_ref, there_ref, own_hbm, payload_ref, weight_ref, position_ref,
    before_hbm, current_hbm, integrals_hbm, denominator_hbm, cat_hbm, new_hbm, send_hbm, own_ref,
    cat_ref, full_ref, left_ref, acc_ref, sem_ref, before_ref, current_ref, integrals_ref,
    denominator_ref, send_ref, even_ref, odd_ref,
):
    pairs, size, unused = denominator_ref.shape
    near = here_ref.shape[0]
    fetches = [
        pltpu.make_async_copy(hbm, ref, sem_ref.at[2 + i])
        for i, (hbm, ref) in enumerate(
            (
                (before_hbm, before_ref), (current_hbm, current_ref),
                (integrals_hbm, integrals_ref), (denominator_hbm, denominator_ref),
            )
        )
    ]

    @pl.when(pl.program_id(0) == 0)
    def fetch():
        for copy in fetches:
            copy.start()

    near_chunk(
        base_ref[0], request_ref, there_ref, own_hbm, payload_ref, weight_ref, position_ref,
        cat_hbm, own_ref, cat_ref, full_ref, left_ref, acc_ref, sem_ref,
    )

    @pl.when(pl.program_id(0) == pl.num_programs(0) - 1)
    def finish():
        for copy in fetches:
            copy.wait()
        for s in range(pairs):
            rows = slice(s * size, (s + 1) * size)
            current, denominator = current_ref[rows, :], denominator_ref[s]
            coupled = coupled_of(acc_ref[s] + before_ref[s])
            residual = integrals_ref[rows, :] + denominator * current - coupled
            new = current - residual / denominator
            current_ref[rows, :] = new
            store_codes(new, even_ref, odd_ref, s)

        far_start = base_ref[0] // 2
        near_start = near - far_start
        column = base_ref[1]

        def pack(n, carry):
            for start, table_ref in ((near_start, here_ref), (far_start, there_ref)):
                first = table_ref[n, 0, column]
                second = table_ref[n, 0, column + 1]
                send_ref[start + n] = even_ref[first] + odd_ref[second]
            return carry

        lax.fori_loop(0, near, pack, 0)
        copies = [
            pltpu.make_async_copy(send_ref, send_hbm, sem_ref.at[2]),
            pltpu.make_async_copy(current_ref, new_hbm, sem_ref.at[3]),
        ]
        for copy in copies:
            copy.start()
        for copy in copies:
            copy.wait()


def second_kernel(
    base_ref, near_cat_hbm, far_cat_hbm, weight_ref, position_ref, amp_ref, current_hbm,
    integrals_hbm, denominator_hbm, new_ref, residual_ref, cat_ref, left_ref, acc_ref,
    current_ref, integrals_ref, denominator_ref, new_rows_ref, residual_rows_ref, sem_ref,
):
    pairs, size, unused = denominator_ref.shape
    step = pl.program_id(0)
    lanes = cat_ref.shape[3]
    slots = lanes // size
    cats = (near_cat_hbm, far_cat_hbm)
    fetches = [
        pltpu.make_async_copy(hbm, ref, sem_ref.at[i])
        for i, (hbm, ref) in enumerate(
            (
                (current_hbm, current_ref), (integrals_hbm, integrals_ref),
                (denominator_hbm, denominator_ref),
            )
        )
    ]
    cut = lanes // CUTS
    copies = [
        [
            pltpu.make_async_copy(
                cats[part].at[step, :, :, pl.ds(i * cut, cut)],
                cat_ref.at[part, :, :, pl.ds(i * cut, cut)],
                sem_ref.at[3 + part * CUTS + i],
            )
            for i in range(CUTS)
        ]
        for part in range(2)
    ]
    for copy in copies[0] + copies[1]:
        copy.start()

    @pl.when(step == 0)
    def fetch():
        for copy in fetches:
            copy.start()

    for part in range(2):
        first = base_ref[part] + step * slots
        weights = slot_weights(first, weight_ref, position_ref, slots, size)
        if part == 0:
            before = lambda s: jnp.where(step == 0, 0.0, acc_ref[s])
        else:
            before = lambda s: acc_ref[s]

        def ready(j, part=part):
            if j * 2 * size % cut == 0:
                copies[part][j * 2 * size // cut].wait()

        sweep_chunk(
            weights, lambda j: parts_of_codes(amp_ref[first // 2 + j]), cat_ref.at[part], left_ref.at[part],
            acc_ref, before, ready,
        )

    @pl.when(step == pl.num_programs(0) - 1)
    def finish():
        for copy in fetches:
            copy.wait()
        for s in range(pairs):
            rows = slice(s * size, (s + 1) * size)
            current, denominator = current_ref[rows, :], denominator_ref[s]
            residual = integrals_ref[rows, :] + denominator * current - coupled_of(acc_ref[s])
            residual_rows_ref[rows, :] = residual
            new_rows_ref[rows, :] = current - residual / denominator
        for rows_ref, out_ref in ((residual_rows_ref, residual_ref), (new_rows_ref, new_ref)):
            for a in range(0, size, 2):
                out_ref[:, a * size : (a + 2) * size] = jnp.concatenate(
                    [rows_ref[pl.ds(a + i, pairs, stride=size), :] for i in range(2)], axis=1
                )


def smem():
    return pl.BlockSpec(memory_space=pltpu.SMEM)


def vmem():
    return pl.BlockSpec(memory_space=pltpu.VMEM)


def hbm():
    return pl.BlockSpec(memory_space=pltpu.HBM)


def in_hbm(*arrays):
    return [pltpu.with_memory_space_constraint(array, pltpu.HBM) for array in arrays]


def by_step(shape, steps):
    if steps == 1:
        return vmem()
    return pl.BlockSpec(shape, lambda i, *refs: (i,) + (0,) * (len(shape) - 1))


def params():
    return pltpu.CompilerParams(
        dimension_semantics=("arbitrary",), vmem_limit_bytes=VMEM_LIMIT
    )


def prepare(pnos, domains, amplitudes, integrals):
    pairs, size, width = pnos.shape
    own = (pairs * size, ATOMS * (width // domains.shape[1]))
    block = (pairs * size, size)
    return pl.pallas_call(
        prepare_kernel,
        in_specs=[vmem()] * 4,
        out_specs=[vmem()] * 3,
        out_shape=[
            pltpu.HBM(own, jnp.bfloat16), pltpu.HBM(block, jnp.float32),
            pltpu.HBM(block, jnp.float32),
        ],
        scratch_shapes=[pltpu.VMEM((pairs, width), jnp.float32)],
        compiler_params=pltpu.CompilerParams(vmem_limit_bytes=VMEM_LIMIT),
        name="prepare",
    )(pnos, domains, amplitudes, integrals)


def pack_payload(column, table, pnos, amplitudes):
    pairs, size, width = pnos.shape
    near = table.shape[0]
    return pl.pallas_call(
        pack_kernel,
        in_specs=[smem(), smem(), vmem(), vmem()],
        out_specs=vmem(),
        out_shape=jax.ShapeDtypeStruct((near, 3 * size, width), jnp.bfloat16),
        scratch_shapes=[
            pltpu.VMEM((pairs * size, size), jnp.float32),
            pltpu.VMEM((pairs, size, 4 * size), jnp.bfloat16),
            pltpu.VMEM((pairs, size, 4 * size), jnp.bfloat16),
        ],
        compiler_params=pltpu.CompilerParams(vmem_limit_bytes=VMEM_LIMIT),
        name="pack_payload",
    )(column, table, pnos, amplitudes)


def chunk_shapes(own, payload, pairs, size):
    near, rows, width = payload.shape
    step = near if near <= ONE_STEP else NEAR_STEP
    lanes = 2 * step * size
    cat = (near // step, pairs, 2 * size, lanes)
    acc = (pairs, 2 * size, 2 * size)
    scratch = [
        pltpu.VMEM(own.shape, jnp.bfloat16),
        pltpu.VMEM(cat[1:], jnp.bfloat16),
        pltpu.VMEM((lanes, own.shape[1]), jnp.bfloat16),
        pltpu.VMEM((pairs, 2 * size, lanes), jnp.bfloat16),
        pltpu.VMEM(acc, jnp.float32),
        pltpu.SemaphoreType.DMA((6,)),
    ]
    return cat, (step, rows, width), acc, scratch


def first_sweep(base, request, table, own, payload, weight, position, size):
    cat, chunk, acc, scratch = chunk_shapes(own, payload, weight.shape[0], size)
    steps = cat[0]
    return pl.pallas_call(
        first_kernel,
        grid=(steps,),
        in_specs=[smem(), smem(), smem(), hbm(), by_step(chunk, steps), vmem(), vmem()],
        out_specs=[hbm(), hbm()],
        out_shape=[
            pltpu.HBM(cat, jnp.bfloat16), pltpu.HBM(acc, jnp.float32)
        ],
        scratch_shapes=scratch,
        compiler_params=params(),
        name="first_sweep_near",
    )(base, request, table, *in_hbm(own), payload, weight, position)


def first_sweep_end(
    base, request, here, there, own, payload, weight, position, before, current, integrals,
    denominator,
):
    pairs, size, unused = denominator.shape
    cat, chunk, acc, scratch = chunk_shapes(own, payload, pairs, size)
    steps = cat[0]
    parts = (pairs, size + CODE_ROWS, 2 * size)
    send = (2 * here.shape[0],) + parts[1:]
    return pl.pallas_call(
        first_end_kernel,
        grid=(steps,),
        in_specs=[smem()] * 4 + [hbm(), by_step(chunk, steps), vmem(), vmem()] + [hbm()] * 4,
        out_specs=[hbm()] * 3,
        out_shape=[
            pltpu.HBM(cat, jnp.bfloat16), pltpu.HBM(current.shape, jnp.float32),
            pltpu.HBM(send, jnp.int16),
        ],
        scratch_shapes=scratch + [
            pltpu.VMEM(acc, jnp.float32),
            pltpu.VMEM(current.shape, jnp.float32),
            pltpu.VMEM(current.shape, jnp.float32),
            pltpu.VMEM(denominator.shape, jnp.float32),
            pltpu.VMEM(send, jnp.int16),
            pltpu.VMEM(parts, jnp.int16),
            pltpu.VMEM(parts, jnp.int16),
        ],
        compiler_params=params(),
        name="first_sweep_far",
    )(
        base, request, here, there, *in_hbm(own), payload, weight, position,
        *in_hbm(before, current, integrals, denominator),
    )


def second_sweep(
    base, near_cat, far_cat, weight, position, amp, current, integrals, denominator
):
    pairs, size, unused = denominator.shape
    steps, lanes = near_cat.shape[0], near_cat.shape[3]
    flat = (pairs, size * size)
    return pl.pallas_call(
        second_kernel,
        grid=(steps,),
        in_specs=[smem(), hbm(), hbm(), vmem(), vmem(), vmem(), hbm(), hbm(), hbm()],
        out_specs=[vmem(), vmem()],
        out_shape=[jax.ShapeDtypeStruct(flat, jnp.float32)] * 2,
        scratch_shapes=[
            pltpu.VMEM((2,) + near_cat.shape[1:], jnp.bfloat16),
            pltpu.VMEM((2, pairs, 2 * size, lanes), jnp.bfloat16),
            pltpu.VMEM((pairs, 2 * size, 2 * size), jnp.float32),
            pltpu.VMEM(current.shape, jnp.float32),
            pltpu.VMEM(current.shape, jnp.float32),
            pltpu.VMEM(denominator.shape, jnp.float32),
            pltpu.VMEM(current.shape, jnp.float32),
            pltpu.VMEM(current.shape, jnp.float32),
            pltpu.SemaphoreType.DMA((3 + 2 * CUTS,)),
        ],
        compiler_params=params(),
        name="second_sweep",
    )(
        base, *in_hbm(near_cat, far_cat), weight, position, amp,
        *in_hbm(current, integrals, denominator),
    )


def on_device(
    amplitudes, integrals, virtual, occupied, coupling, degree, position, request, pnos, domains
):
    pairs = amplitudes.shape[0]
    size = virtual.shape[1]
    depth = coupling.shape[1]
    width = pnos.shape[2]
    slots = request.shape[1]
    near = slots // 4
    half = lax.axis_index("half").astype(jnp.int32)
    mine = lax.axis_index("near").astype(jnp.int32)
    swap = [(0, 1), (1, 0)]

    far_pnos = lax.ppermute(pnos, "half", swap)
    far_amplitudes = lax.ppermute(amplitudes, "half", swap)
    near_base = half * 2 * near
    far_base = (1 - half) * 2 * near
    near_column = near_base + 2 * mine
    far_column = far_base + 2 * mine

    def near_exchange(request, pnos, amplitudes, domains):
        row = jnp.concatenate([request, domains.reshape(1, -1)], axis=1)
        here = jnp.broadcast_to(row[None], (near, 1, row.shape[1]))
        here = lax.all_to_all(here, "near", split_axis=0, concat_axis=0, tiled=True)
        there = lax.ppermute(here, "half", swap)
        outgoing = pack_payload(near_column.reshape(1), here, pnos, amplitudes)
        payload = lax.all_to_all(outgoing, "near", split_axis=0, concat_axis=0, tiled=True)
        return here, there, payload

    def no_exchange(request, pnos, amplitudes, domains):
        table = jnp.zeros((near, 1, slots + domains.size), jnp.int32)
        return table, table, jnp.zeros((near, 3 * size, width), jnp.bfloat16)

    here, there, near_payload = lax.cond(
        degree[0] > 0, near_exchange, no_exchange, request, pnos, amplitudes, domains
    )
    outgoing = pack_payload(far_column.reshape(1), here, far_pnos, far_amplitudes)
    far_payload = lax.all_to_all(outgoing, "near", split_axis=0, concat_axis=0, tiled=True)

    live = jnp.arange(depth, dtype=jnp.int32)[None, :] < degree[:, None]
    weight = jnp.where(live, coupling, jnp.zeros_like(coupling))
    denominator = virtual[:, :, None] + virtual[:, None, :] - occupied[:, None, None]
    own, current, integrals = prepare(pnos, domains, amplitudes, integrals)
    near_cat, before = first_sweep(
        near_base.reshape(1), request, here, own, near_payload, weight, position, size
    )
    far_cat, current, amp = first_sweep_end(
        jnp.stack([far_base, near_column]), request, here, there, own, far_payload, weight,
        position, before, current, integrals, denominator,
    )
    amp = lax.all_to_all(amp, ("half", "near"), split_axis=0, concat_axis=0, tiled=True)
    new, residual = second_sweep(
        jnp.stack([near_base, far_base]), near_cat, far_cat, weight, position, amp, current,
        integrals, denominator,
    )
    return new, residual


def solution(mesh):
    count = mesh.shape["pair"]
    devices = mesh.devices.reshape(mesh.shape["frag"], 2, count // 2)
    split_mesh = Mesh(devices, ("frag", "half", "near"))
    rows = ("frag", "half", "near")
    return jax.shard_map(
        on_device,
        mesh=split_mesh,
        in_specs=(
            P(rows, None), P(rows, None), P(rows, None), P(rows), P(rows, None),
            P(rows), P(rows, None), P(rows, None), P(rows, None, None), P(rows, None),
        ),
        out_specs=(P(rows, None), P(rows, None)),
        check_vma=False,
    )
```

```python
import jax
import jax.numpy as jnp
from jax import lax
from jax.experimental import pallas as pl
from jax.experimental.pallas import tpu as pltpu
from jax.sharding import Mesh, PartitionSpec as P

ATOMS = 32
CHUNK = 4
ONE_STEP = 16
LOG_TOP = 125.0
CODE_TOP = 32767.0
CODE_ROWS = 16
AHEAD = 2
SMALLEST = 2.0**-100
VMEM_LIMIT = 32 * 1024 * 1024
NT = (((1,), (1,)), ((), ()))


def split(value):
    high = value.astype(jnp.bfloat16)
    low = (value - high.astype(jnp.float32)).astype(jnp.bfloat16)
    return high, low


def scale_of(eighths):
    return jnp.exp2(eighths * 0.125)


def eighths_of(value):
    top = jnp.maximum(jnp.max(jnp.abs(value), axis=0, keepdims=True), SMALLEST)
    return jnp.ceil(jnp.log2(top) * 8.0)


def store_codes(value, even_ref, odd_ref, p):
    size = value.shape[0]
    eighths = eighths_of(value)
    codes = jnp.clip(jnp.round(value * (CODE_TOP / scale_of(eighths))), -CODE_TOP, CODE_TOP)
    rows = jnp.concatenate([codes, jnp.broadcast_to(eighths, (CODE_ROWS, size))], axis=0)
    blank = jnp.zeros_like(rows)
    for ref, parts in ((even_ref, [rows, blank]), (odd_ref, [blank, rows])):
        ref[p] = jnp.concatenate(parts, axis=1).astype(jnp.int32).astype(jnp.int16)


def block_of_codes(codes):
    rows = codes.astype(jnp.int32).astype(jnp.float32)
    size = rows.shape[0] - CODE_ROWS
    return rows[:size, :] * (scale_of(rows[size : size + 1, :]) * (1.0 / CODE_TOP))


def log_code(value, eighths):
    power = jnp.clip(value * (LOG_TOP / scale_of(eighths)), -LOG_TOP, LOG_TOP)
    return jnp.exp2(power)


def block_of_logs(logs, eighths):
    rows, lanes = logs.shape[0], logs.shape[1] // 2
    size = lanes // 2
    first, second = logs[:, :lanes], logs[:, lanes:]
    left = lax.broadcasted_iota(jnp.int32, (rows, lanes), 1) < size
    upper = jnp.where(left, first, pltpu.roll(second, size, 1))
    lower = jnp.where(left, pltpu.roll(first, size, 1), second)
    both = jnp.concatenate([upper, lower], axis=0)
    return jnp.log2(both) * (scale_of(eighths) * (1.0 / LOG_TOP))


def to_blocks(flat_ref, rows_ref, size):
    pairs = flat_ref.shape[0]
    for a in range(0, size, 2):
        both = flat_ref[:, a * size : (a + 2) * size]
        rows_ref[pl.ds(a, pairs, stride=size), :] = both[:, :size]
        rows_ref[pl.ds(a + 1, pairs, stride=size), :] = both[:, size:]


def atoms_of_columns(domains, width):
    count = domains.shape[1]
    entry = lax.broadcasted_iota(jnp.int32, (count, width), 0)
    column = lax.broadcasted_iota(jnp.int32, (count, width), 1)
    spread = (entry == column // (width // count)).astype(jnp.float32).astype(jnp.bfloat16)
    atoms = domains.astype(jnp.float32).astype(jnp.bfloat16)
    return jnp.dot(atoms, spread, preferred_element_type=jnp.float32)


def column_table(atoms, columns):
    width = atoms.shape[1]
    per_atom = columns // ATOMS
    row = lax.broadcasted_iota(jnp.int32, (columns, width), 0)
    column = lax.broadcasted_iota(jnp.int32, (1, width), 1)
    ids = atoms.astype(jnp.int32) * per_atom + column % per_atom
    return (row == ids).astype(jnp.float32).astype(jnp.bfloat16)


def prepare_kernel(
    pnos_ref, domains_ref, amp_ref, integrals_ref, own_ref, current_ref, blocks_ref, atoms_ref
):
    pairs, size, width = pnos_ref.shape
    columns = own_ref.shape[1]
    to_blocks(amp_ref, current_ref, size)
    to_blocks(integrals_ref, blocks_ref, size)
    atoms_ref[...] = atoms_of_columns(domains_ref[...], width)
    for p in range(pairs):
        own_ref[p * size : (p + 1) * size, :] = lax.dot_general(
            pnos_ref[p], column_table(atoms_ref[p : p + 1, :], columns), NT,
            preferred_element_type=jnp.float32,
        ).astype(jnp.bfloat16)


def encode_kernel(
    amp_hbm, domains_hbm, request_hbm, logs_ref, table_ref, amp_ref, domains_ref, request_ref,
    rows_ref, sem_ref,
):
    pairs, half_size, lanes = logs_ref.shape
    size = lanes // 2
    copies = [
        pltpu.make_async_copy(amp_hbm, amp_ref, sem_ref.at[0]),
        pltpu.make_async_copy(domains_hbm, domains_ref, sem_ref.at[1]),
        pltpu.make_async_copy(request_hbm, request_ref, sem_ref.at[2]),
    ]
    for copy in copies:
        copy.start()
    for copy in copies:
        copy.wait()
    to_blocks(amp_ref, rows_ref, size)
    scales = []
    for p in range(pairs):
        block = rows_ref[p * size : (p + 1) * size, :]
        eighths = eighths_of(block)
        logs = log_code(block, eighths)
        logs_ref[p] = jnp.concatenate(
            [logs[:half_size, :], logs[half_size:, :]], axis=1
        ).astype(jnp.bfloat16)
        scales.append(eighths)
    scales = jnp.concatenate(scales, axis=0).astype(jnp.int32)
    count = domains_ref.shape[1]
    slots = request_ref.shape[1]
    table_ref[:, :size] = scales
    table_ref[:, size : size + count] = domains_ref[...]
    table_ref[:, size + count :] = jnp.broadcast_to(request_ref[...], (pairs, slots))


def pack_kernel(
    here_ref, there_ref, pnos_ref, logs_ref, far_pnos_ref, far_logs_ref, out_ref
):
    unused, size, width = pnos_ref.shape
    lanes = logs_ref.shape[2]

    def pack(n, carry):
        parts = ((here_ref, pnos_ref, logs_ref), (there_ref, far_pnos_ref, far_logs_ref))
        for part, (wanted_ref, blocks_ref, codes_ref) in enumerate(parts):
            first = wanted_ref[n, 0]
            second = wanted_ref[n, 1]
            out_ref[n, part, :size] = blocks_ref[first]
            out_ref[n, part, size : 2 * size] = blocks_ref[second]
            out_ref[n, part, 2 * size :, :lanes] = codes_ref[first]
            out_ref[n, part, 2 * size :, lanes:] = codes_ref[second]
        return carry

    lax.fori_loop(0, out_ref.shape[0], pack, 0)


def source_of(entry, half, near):
    return (entry % 2 + half) % 2 * near + entry // 2


def slot_weights(half, near, start, weight_ref, position_ref, size):
    slot = lax.broadcasted_iota(jnp.int32, (1, 2 * CHUNK * size), 1) // size
    source = source_of(start + slot // 2, half, near)
    named = source * 2 + slot % 2
    total = jnp.zeros((weight_ref.shape[0], named.shape[1]), jnp.float32)
    for c in range(weight_ref.shape[1]):
        hit = position_ref[:, c : c + 1] == named
        total += jnp.where(hit, weight_ref[:, c : c + 1], 0.0)
    return total


def half_products(weights, amps, cat_ref, left_ref):
    pairs, rows2, lanes = cat_ref.shape
    size = rows2 // 2
    group = lax.broadcasted_iota(jnp.int32, (size, 4 * size), 1) // size
    even = (group % 2 == 0).astype(jnp.float32).astype(jnp.bfloat16)
    odd = (group % 2 == 1).astype(jnp.float32).astype(jnp.bfloat16)
    for j in range(CHUNK):
        cols = slice(j * 2 * size, (j + 1) * 2 * size)
        amp = jnp.concatenate(split(amps(j)), axis=1)
        first, second = amp * even, amp * odd
        right = jnp.concatenate([first, second, first, second], axis=0)
        high = cat_ref[:, :size, cols].reshape(pairs * size, 2 * size)
        low = cat_ref[:, size:, cols].reshape(pairs * size, 2 * size)
        both = jnp.dot(
            jnp.concatenate([high, low], axis=1), right, preferred_element_type=jnp.float32
        )
        left = (both[:, : 2 * size] + both[:, 2 * size :]).reshape(pairs, size, 2 * size)
        left = left * weights[:, cols].reshape(pairs, 1, 2 * size)
        left_high, left_low = split(left)
        left_ref[:, :size, cols] = left_high
        left_ref[:, size:, cols] = left_low


def add_products(first, cat_ref, left_ref, acc_ref):
    for s in range(acc_ref.shape[0]):
        total = jnp.where(first, 0.0, acc_ref[s])
        for c in range(cat_ref.shape[0]):
            total += lax.dot_general(
                left_ref[c, s], cat_ref[c, s], NT, preferred_element_type=jnp.float32
            )
        acc_ref[s] = total


def cross_chunk(atoms, own_ref, payload_ref, cat_ref, full_ref):
    columns = own_ref.shape[1]
    pairs, rows2, unused = cat_ref.shape
    size = rows2 // 2
    for k in range(2 * CHUNK):
        n, c = k // 2, k % 2
        full_ref[k * size : (k + 1) * size, :] = lax.dot_general(
            payload_ref[n, c * size : (c + 1) * size, :],
            column_table(atoms[k : k + 1, :], columns), NT, preferred_element_type=jnp.float32,
        ).astype(jnp.bfloat16)
    cross = lax.dot_general(own_ref[...], full_ref[...], NT, preferred_element_type=jnp.float32)
    high, low = split(cross)
    cat_ref[:, :size, :] = high.reshape(pairs, size, -1)
    cat_ref[:, size:, :] = low.reshape(pairs, size, -1)


def coupled_of(acc):
    size = acc.shape[0] // 2
    rows = acc[:size] + acc[size:]
    return rows[:, :size] + rows[:, size:]


def first_kernel(
    half_ref, request_ref, wanted_ref, table_ref, own_hbm, payload_ref, weight_ref, position_ref,
    current_hbm, integrals_hbm, denominator_hbm, cat_hbm, new_hbm, send_hbm, own_ref, cat_ref,
    full_ref, left_ref, acc_ref, info_ref, current_ref, integrals_ref, denominator_ref, send_ref,
    even_ref, odd_ref, sem_ref, cat_sem_ref,
):
    pairs, size, unused = denominator_ref.shape
    width = payload_ref.shape[2]
    chunks = cat_ref.shape[0]
    near = wanted_ref.shape[0] // 2
    half = half_ref[0]
    step = pl.program_id(0)
    count = table_ref.shape[2] - size - request_ref.shape[1]
    fetches = [
        pltpu.make_async_copy(hbm, ref, sem_ref.at[i])
        for i, (hbm, ref) in enumerate(
            (
                (own_hbm, own_ref), (current_hbm, current_ref), (integrals_hbm, integrals_ref),
                (denominator_hbm, denominator_ref),
            )
        )
    ]

    @pl.when(step == 0)
    def fetch():
        for copy in fetches:
            copy.start()

    entries = CHUNK * chunks
    lanes = table_ref.shape[2]
    for k in range(2 * entries):
        source = source_of(step * entries + k // 2, half, near)
        row = request_ref[0, source * 2 + k % 2]
        info_ref[k : k + 1, :lanes] = table_ref[source, pl.ds(row, 1), :lanes]
    atoms = atoms_of_columns(info_ref[:, size : size + count], width)
    scales = info_ref[:, : 2 * size].astype(jnp.float32)
    moved = pltpu.roll(scales, size, 1)
    left_lanes = lax.broadcasted_iota(jnp.int32, (1, 2 * size), 1) < size

    @pl.when(step == 0)
    def own_ready():
        fetches[0].wait()

    cat_copies = []
    for c in range(chunks):
        blocks = payload_ref.at[pl.ds(c * CHUNK, CHUNK)]
        cross_chunk(
            atoms[c * 2 * CHUNK : (c + 1) * 2 * CHUNK], own_ref, blocks, cat_ref.at[c],
            full_ref.at[c],
        )
        copy = pltpu.make_async_copy(
            cat_ref.at[c], cat_hbm.at[step * chunks + c], cat_sem_ref.at[c]
        )
        copy.start()
        cat_copies.append(copy)
        start = step * entries + c * CHUNK
        weights = slot_weights(half, near, start, weight_ref, position_ref, size)

        def amps(j, c=c, blocks=blocks):
            k = 2 * (c * CHUNK + j)
            eighths = jnp.where(left_lanes, scales[k : k + 1, :], moved[k + 1 : k + 2, :])
            logs = blocks[j, 2 * size :, :].astype(jnp.float32)
            return block_of_logs(logs, eighths)

        half_products(weights, amps, cat_ref.at[c], left_ref.at[c])
    add_products(step == 0, cat_ref, left_ref, acc_ref)

    @pl.when(step == pl.num_programs(0) - 1)
    def finish():
        for copy in fetches[1:]:
            copy.wait()
        for s in range(pairs):
            rows = slice(s * size, (s + 1) * size)
            current, denominator = current_ref[rows, :], denominator_ref[s]
            residual = integrals_ref[rows, :] + denominator * current - coupled_of(acc_ref[s])
            new = current - residual / denominator
            current_ref[rows, :] = new
            store_codes(new, even_ref, odd_ref, s)

        def pack(d, carry):
            send_ref[d] = even_ref[wanted_ref[d, 0]] + odd_ref[wanted_ref[d, 1]]
            return carry

        lax.fori_loop(0, send_ref.shape[0], pack, 0)
        copies = [
            pltpu.make_async_copy(send_ref, send_hbm, sem_ref.at[0]),
            pltpu.make_async_copy(current_ref, new_hbm, sem_ref.at[1]),
        ]
        for copy in copies:
            copy.start()
        for copy in copies:
            copy.wait()

    for copy in cat_copies:
        copy.wait()


def second_kernel(
    half_ref, cat_hbm, weight_ref, position_ref, amp_ref, current_hbm, integrals_hbm,
    denominator_hbm, new_ref, residual_ref, cat_ref, left_ref, acc_ref, current_ref,
    integrals_ref, denominator_ref, new_rows_ref, residual_rows_ref, sem_ref, cat_sem_ref,
):
    pairs, size, unused = denominator_ref.shape
    step = pl.program_id(0)
    half = half_ref[0]
    near = amp_ref.shape[0] // 2
    chunks = cat_ref.shape[0]
    fetches = [
        pltpu.make_async_copy(hbm, ref, sem_ref.at[i])
        for i, (hbm, ref) in enumerate(
            (
                (current_hbm, current_ref), (integrals_hbm, integrals_ref),
                (denominator_hbm, denominator_ref),
            )
        )
    ]
    copies = [
        pltpu.make_async_copy(
            cat_hbm.at[step * chunks + c], cat_ref.at[c], cat_sem_ref.at[c]
        )
        for c in range(chunks)
    ]
    for copy in copies[:AHEAD]:
        copy.start()
    for c in range(chunks):
        start = (step * chunks + c) * CHUNK
        weights = slot_weights(half, near, start, weight_ref, position_ref, size)
        copies[c].wait()
        if c + AHEAD < chunks:
            copies[c + AHEAD].start()
        elif c + AHEAD == chunks or c == chunks - 1 and chunks < AHEAD:
            @pl.when(step == pl.num_programs(0) - 1)
            def fetch():
                for copy in fetches:
                    copy.start()

        half_products(
            weights, lambda j: block_of_codes(amp_ref[source_of(start + j, half, near)]),
            cat_ref.at[c], left_ref.at[c],
        )
    add_products(step == 0, cat_ref, left_ref, acc_ref)

    @pl.when(step == pl.num_programs(0) - 1)
    def finish():
        for copy in fetches:
            copy.wait()
        for s in range(pairs):
            rows = slice(s * size, (s + 1) * size)
            current, denominator = current_ref[rows, :], denominator_ref[s]
            residual = integrals_ref[rows, :] + denominator * current - coupled_of(acc_ref[s])
            residual_rows_ref[rows, :] = residual
            new_rows_ref[rows, :] = current - residual / denominator
        for rows_ref, out_ref in ((residual_rows_ref, residual_ref), (new_rows_ref, new_ref)):
            for a in range(0, size, 2):
                out_ref[:, a * size : (a + 2) * size] = jnp.concatenate(
                    [rows_ref[pl.ds(a + i, pairs, stride=size), :] for i in range(2)], axis=1
                )


def smem():
    return pl.BlockSpec(memory_space=pltpu.SMEM)


def vmem():
    return pl.BlockSpec(memory_space=pltpu.VMEM)


def hbm():
    return pl.BlockSpec(memory_space=pltpu.HBM)


def in_hbm(*arrays):
    return [pltpu.with_memory_space_constraint(array, pltpu.HBM) for array in arrays]


def params():
    return pltpu.CompilerParams(
        dimension_semantics=("arbitrary",), vmem_limit_bytes=VMEM_LIMIT
    )


def limit():
    return pltpu.CompilerParams(vmem_limit_bytes=VMEM_LIMIT)


def prepare(pnos, domains, amplitudes, integrals):
    pairs, size, width = pnos.shape
    own = (pairs * size, ATOMS * (width // domains.shape[1]))
    block = (pairs * size, size)
    return pl.pallas_call(
        prepare_kernel,
        in_specs=[vmem()] * 4,
        out_specs=[vmem()] * 3,
        out_shape=[
            pltpu.HBM(own, jnp.bfloat16), pltpu.HBM(block, jnp.float32),
            pltpu.HBM(block, jnp.float32),
        ],
        scratch_shapes=[pltpu.VMEM((pairs, width), jnp.float32)],
        compiler_params=limit(),
        name="prepare",
    )(pnos, domains, amplitudes, integrals)


def encode(amplitudes, domains, request, size):
    pairs = amplitudes.shape[0]
    lanes = size + domains.shape[1] + request.shape[1]
    return pl.pallas_call(
        encode_kernel,
        in_specs=[hbm()] * 3,
        out_specs=[vmem()] * 2,
        out_shape=[
            jax.ShapeDtypeStruct((pairs, size // 2, 2 * size), jnp.bfloat16),
            jax.ShapeDtypeStruct((pairs, lanes), jnp.int32),
        ],
        scratch_shapes=[
            pltpu.VMEM(amplitudes.shape, jnp.float32), pltpu.VMEM(domains.shape, jnp.int32),
            pltpu.VMEM(request.shape, jnp.int32), pltpu.VMEM((pairs * size, size), jnp.float32),
            pltpu.SemaphoreType.DMA((3,)),
        ],
        compiler_params=limit(),
        name="encode",
    )(*in_hbm(amplitudes, domains, request))


def pack_payload(here, there, pnos, logs, far_pnos, far_logs):
    unused, size, width = pnos.shape
    rows = 2 * size + logs.shape[1]
    return pl.pallas_call(
        pack_kernel,
        in_specs=[smem(), smem()] + [vmem()] * 4,
        out_specs=vmem(),
        out_shape=jax.ShapeDtypeStruct((here.shape[0], 2, rows, width), jnp.bfloat16),
        compiler_params=limit(),
        name="pack_payload",
    )(here, there, pnos, logs, far_pnos, far_logs)


def sweep_shapes(entries, pairs, size):
    chunks = entries // CHUNK if entries <= ONE_STEP else 1
    cat = (entries // CHUNK, pairs, 2 * size, 2 * CHUNK * size)
    held = (chunks,) + cat[1:]
    scratch = [
        pltpu.VMEM(held, jnp.bfloat16), pltpu.VMEM(held, jnp.bfloat16),
        pltpu.VMEM((pairs, 2 * size, 2 * size), jnp.float32),
    ]
    return cat[0] // chunks, chunks, cat, scratch


def first_sweep(
    half, request, wanted, table, own, payload, weight, position, current, integrals, denominator
):
    pairs, size, unused = denominator.shape
    entries, rows, width = payload.shape
    steps, chunks, cat, (cats, lefts, acc) = sweep_shapes(entries, pairs, size)
    block = (CHUNK * chunks, rows, width)
    blocks = vmem() if steps == 1 else pl.BlockSpec(block, lambda i: (i, 0, 0))
    parts = (pairs, size + CODE_ROWS, 2 * size)
    send = (entries,) + parts[1:]
    return pl.pallas_call(
        first_kernel,
        grid=(steps,),
        in_specs=[smem()] * 3 + [vmem(), hbm(), blocks, vmem(), vmem()] + [hbm()] * 3,
        out_specs=[hbm()] * 3,
        out_shape=[
            pltpu.HBM(cat, jnp.bfloat16), pltpu.HBM(current.shape, jnp.float32),
            pltpu.HBM(send, jnp.int16),
        ],
        scratch_shapes=[
            pltpu.VMEM(own.shape, jnp.bfloat16),
            cats,
            pltpu.VMEM((chunks, cat[3], own.shape[1]), jnp.bfloat16),
            lefts,
            acc,
            pltpu.VMEM((2 * CHUNK * chunks, max(table.shape[2], 2 * size)), jnp.int32),
            pltpu.VMEM(current.shape, jnp.float32),
            pltpu.VMEM(current.shape, jnp.float32),
            pltpu.VMEM(denominator.shape, jnp.float32),
            pltpu.VMEM(send, jnp.int16),
            pltpu.VMEM(parts, jnp.int16),
            pltpu.VMEM(parts, jnp.int16),
            pltpu.SemaphoreType.DMA((4,)),
            pltpu.SemaphoreType.DMA((chunks,)),
        ],
        compiler_params=params(),
        name="first_sweep",
    )(
        half, request, wanted, table, *in_hbm(own), payload, weight, position,
        *in_hbm(current, integrals, denominator),
    )


def second_sweep(half, cat, weight, position, amp, current, integrals, denominator):
    pairs, size, unused = denominator.shape
    steps, chunks, unused, scratch = sweep_shapes(amp.shape[0], pairs, size)
    flat = (pairs, size * size)
    return pl.pallas_call(
        second_kernel,
        grid=(steps,),
        in_specs=[smem(), hbm(), vmem(), vmem(), vmem(), hbm(), hbm(), hbm()],
        out_specs=[vmem(), vmem()],
        out_shape=[jax.ShapeDtypeStruct(flat, jnp.float32)] * 2,
        scratch_shapes=scratch + [
            pltpu.VMEM(current.shape, jnp.float32),
            pltpu.VMEM(current.shape, jnp.float32),
            pltpu.VMEM(denominator.shape, jnp.float32),
            pltpu.VMEM(current.shape, jnp.float32),
            pltpu.VMEM(current.shape, jnp.float32),
            pltpu.SemaphoreType.DMA((3,)),
            pltpu.SemaphoreType.DMA((chunks,)),
        ],
        compiler_params=params(),
        name="second_sweep",
    )(
        half, *in_hbm(cat), weight, position, amp, *in_hbm(current, integrals, denominator),
    )


def on_device(
    amplitudes, integrals, virtual, occupied, coupling, degree, position, request, pnos, domains
):
    pairs = amplitudes.shape[0]
    size = virtual.shape[1]
    depth = coupling.shape[1]
    slots = request.shape[1]
    entries = slots // 2
    near = entries // 2
    half = lax.axis_index("half").astype(jnp.int32)
    mine = lax.axis_index("near").astype(jnp.int32)
    swap = [(0, 1), (1, 0)]
    both = ("half", "near")

    far_pnos = lax.ppermute(pnos, "half", swap)
    logs, table = encode(amplitudes, domains, request, size)
    far_logs = lax.ppermute(logs, "half", swap)

    def gather(row):
        rows = jnp.broadcast_to(row[None], (entries,) + row.shape)
        return lax.all_to_all(rows, both, split_axis=0, concat_axis=0, tiled=True)

    def nothing(row):
        return jnp.zeros((entries,) + row.shape, jnp.int32)

    table = lax.cond(degree[0] > 0, gather, nothing, table)
    column = table.shape[2] - slots + 2 * mine
    wanted = lax.dynamic_slice(
        table, (0, 0, column + half * 2 * near), (entries, 1, 2)
    ).reshape(entries, 2)
    here = lax.dynamic_slice(wanted, (half * near, 0), (near, 2))
    there = lax.dynamic_slice(
        table, (half * near, 0, column + (1 - half) * 2 * near), (near, 1, 2)
    ).reshape(near, 2)

    payload = pack_payload(here, there, pnos, logs, far_pnos, far_logs)
    payload = lax.all_to_all(payload, "near", split_axis=0, concat_axis=0, tiled=True)
    payload = payload.reshape((entries,) + payload.shape[2:])

    live = jnp.arange(depth, dtype=jnp.int32)[None, :] < degree[:, None]
    weight = jnp.where(live, coupling, jnp.zeros_like(coupling))
    denominator = virtual[:, :, None] + virtual[:, None, :] - occupied[:, None, None]
    own, current, integrals = prepare(pnos, domains, amplitudes, integrals)
    half = half.reshape(1)
    cat, current, amp = first_sweep(
        half, request, wanted, table, own, payload, weight, position, current, integrals,
        denominator,
    )
    amp = lax.all_to_all(amp, both, split_axis=0, concat_axis=0, tiled=True)
    new, residual = second_sweep(
        half, cat, weight, position, amp, current, integrals, denominator
    )
    return new, residual


def solution(mesh):
    count = mesh.shape["pair"]
    devices = mesh.devices.reshape(mesh.shape["frag"], 2, count // 2)
    split_mesh = Mesh(devices, ("frag", "half", "near"))
    rows = ("frag", "half", "near")
    return jax.shard_map(
        on_device,
        mesh=split_mesh,
        in_specs=(
            P(rows, None), P(rows, None), P(rows, None), P(rows), P(rows, None),
            P(rows), P(rows, None), P(rows, None), P(rows, None, None), P(rows, None),
        ),
        out_specs=(P(rows, None), P(rows, None)),
        check_vma=False,
    )
```

```python
import jax
import jax.numpy as jnp
from jax import lax
from jax.experimental import pallas as pl
from jax.experimental.pallas import tpu as pltpu
from jax.sharding import Mesh, PartitionSpec as P

ATOMS = 32
CHUNK = 4
ONE_STEP = 16
LOG_TOP = 125.0
CODE_TOP = 32767.0
CODE_ROWS = 16
SMALLEST = 2.0**-100
VMEM_LIMIT = 32 * 1024 * 1024
NT = (((1,), (1,)), ((), ()))


def split(value):
    high = value.astype(jnp.bfloat16)
    low = (value - high.astype(jnp.float32)).astype(jnp.bfloat16)
    return high, low


def scale_of(eighths):
    return jnp.exp2(eighths * 0.125)


def eighths_of(value):
    top = jnp.maximum(jnp.max(jnp.abs(value), axis=0, keepdims=True), SMALLEST)
    return jnp.ceil(jnp.log2(top) * 8.0)


def store_codes(value, even_ref, odd_ref, p):
    size = value.shape[0]
    eighths = eighths_of(value)
    codes = jnp.clip(jnp.round(value * (CODE_TOP / scale_of(eighths))), -CODE_TOP, CODE_TOP)
    rows = jnp.concatenate([codes, jnp.broadcast_to(eighths, (CODE_ROWS, size))], axis=0)
    blank = jnp.zeros_like(rows)
    for ref, parts in ((even_ref, [rows, blank]), (odd_ref, [blank, rows])):
        ref[p] = jnp.concatenate(parts, axis=1).astype(jnp.int32).astype(jnp.int16)


def block_of_codes(codes):
    rows = codes.astype(jnp.int32).astype(jnp.float32)
    size = rows.shape[0] - CODE_ROWS
    return rows[:size, :] * (scale_of(rows[size : size + 1, :]) * (1.0 / CODE_TOP))


def log_code(value, eighths):
    power = jnp.clip(value * (LOG_TOP / scale_of(eighths)), -LOG_TOP, LOG_TOP)
    return jnp.exp2(power)


def block_of_logs(logs, eighths):
    rows, lanes = logs.shape[0], logs.shape[1] // 2
    size = lanes // 2
    first, second = logs[:, :lanes], logs[:, lanes:]
    left = lax.broadcasted_iota(jnp.int32, (rows, lanes), 1) < size
    upper = jnp.where(left, first, pltpu.roll(second, size, 1))
    lower = jnp.where(left, pltpu.roll(first, size, 1), second)
    both = jnp.concatenate([upper, lower], axis=0)
    return jnp.log2(both) * (scale_of(eighths) * (1.0 / LOG_TOP))


def to_blocks(flat_ref, rows_ref, size):
    pairs = flat_ref.shape[0]
    for a in range(0, size, 2):
        both = flat_ref[:, a * size : (a + 2) * size]
        rows_ref[pl.ds(a, pairs, stride=size), :] = both[:, :size]
        rows_ref[pl.ds(a + 1, pairs, stride=size), :] = both[:, size:]


def atoms_of_columns(domains, width):
    count = domains.shape[1]
    entry = lax.broadcasted_iota(jnp.int32, (count, width), 0)
    column = lax.broadcasted_iota(jnp.int32, (count, width), 1)
    spread = (entry == column // (width // count)).astype(jnp.float32).astype(jnp.bfloat16)
    atoms = domains.astype(jnp.float32).astype(jnp.bfloat16)
    return jnp.dot(atoms, spread, preferred_element_type=jnp.float32)


def column_table(atoms, columns):
    width = atoms.shape[1]
    per_atom = columns // ATOMS
    row = lax.broadcasted_iota(jnp.int32, (columns, width), 0).astype(jnp.int16)
    column = lax.broadcasted_iota(jnp.int32, (1, width), 1)
    ids = (atoms.astype(jnp.int32) * per_atom + column % per_atom).astype(jnp.int16)
    return jnp.where(row == ids, jnp.ones((), jnp.bfloat16), jnp.zeros((), jnp.bfloat16))


def prepare_kernel(
    pnos_ref, domains_ref, amp_ref, integrals_ref, own_ref, current_ref, blocks_ref, atoms_ref
):
    pairs, size, width = pnos_ref.shape
    columns = own_ref.shape[1]
    to_blocks(amp_ref, current_ref, size)
    to_blocks(integrals_ref, blocks_ref, size)
    atoms_ref[...] = atoms_of_columns(domains_ref[...], width)
    for p in range(pairs):
        own_ref[p * size : (p + 1) * size, :] = lax.dot_general(
            pnos_ref[p], column_table(atoms_ref[p : p + 1, :], columns), NT,
            preferred_element_type=jnp.float32,
        ).astype(jnp.bfloat16)


def encode_kernel(
    amp_hbm, domains_hbm, request_hbm, logs_ref, table_ref, amp_ref, domains_ref, request_ref,
    rows_ref, sem_ref,
):
    pairs, half_size, lanes = logs_ref.shape
    size = lanes // 2
    copies = [
        pltpu.make_async_copy(amp_hbm, amp_ref, sem_ref.at[0]),
        pltpu.make_async_copy(domains_hbm, domains_ref, sem_ref.at[1]),
        pltpu.make_async_copy(request_hbm, request_ref, sem_ref.at[2]),
    ]
    for copy in copies:
        copy.start()
    for copy in copies:
        copy.wait()
    to_blocks(amp_ref, rows_ref, size)
    scales = []
    for p in range(pairs):
        block = rows_ref[p * size : (p + 1) * size, :]
        eighths = eighths_of(block)
        logs = log_code(block, eighths)
        logs_ref[p] = jnp.concatenate(
            [logs[:half_size, :], logs[half_size:, :]], axis=1
        ).astype(jnp.bfloat16)
        scales.append(eighths)
    scales = jnp.concatenate(scales, axis=0).astype(jnp.int32)
    count = domains_ref.shape[1]
    slots = request_ref.shape[1]
    table_ref[:, :size] = scales
    table_ref[:, size : size + count] = domains_ref[...]
    table_ref[:, size + count :] = jnp.broadcast_to(request_ref[...], (pairs, slots))


def pack_kernel(
    here_ref, there_ref, pnos_ref, logs_ref, far_pnos_ref, far_logs_ref, out_ref
):
    unused, size, width = pnos_ref.shape
    lanes = logs_ref.shape[2]

    def pack(n, carry):
        parts = ((here_ref, pnos_ref, logs_ref), (there_ref, far_pnos_ref, far_logs_ref))
        for part, (wanted_ref, blocks_ref, codes_ref) in enumerate(parts):
            first = wanted_ref[n, 0]
            second = wanted_ref[n, 1]
            out_ref[n, part, :size] = blocks_ref[first]
            out_ref[n, part, size : 2 * size] = blocks_ref[second]
            out_ref[n, part, 2 * size :, :lanes] = codes_ref[first]
            out_ref[n, part, 2 * size :, lanes:] = codes_ref[second]
        return carry

    lax.fori_loop(0, out_ref.shape[0], pack, 0)


def source_of(entry, half, near):
    return (entry % 2 + half) % 2 * near + entry // 2


def slot_weights(half, near, start, weight_ref, position_ref, size):
    slot = lax.broadcasted_iota(jnp.int32, (1, 2 * CHUNK * size), 1) // size
    source = source_of(start + slot // 2, half, near)
    named = source * 2 + slot % 2
    total = jnp.zeros((weight_ref.shape[0], named.shape[1]), jnp.float32)
    for c in range(weight_ref.shape[1]):
        hit = position_ref[:, c : c + 1] == named
        total += jnp.where(hit, weight_ref[:, c : c + 1], 0.0)
    return total


def half_products(weights, amps, cat_ref, left_ref):
    pairs, rows2, lanes = cat_ref.shape
    size = rows2 // 2
    group = lax.broadcasted_iota(jnp.int32, (size, 4 * size), 1) // size
    even = (group % 2 == 0).astype(jnp.float32).astype(jnp.bfloat16)
    odd = (group % 2 == 1).astype(jnp.float32).astype(jnp.bfloat16)
    for j in range(CHUNK):
        cols = slice(j * 2 * size, (j + 1) * 2 * size)
        amp = jnp.concatenate(split(amps(j)), axis=1)
        first, second = amp * even, amp * odd
        right = jnp.concatenate([first, second, first, second], axis=0)
        high = cat_ref[:, :size, cols].reshape(pairs * size, 2 * size)
        low = cat_ref[:, size:, cols].reshape(pairs * size, 2 * size)
        both = jnp.dot(
            jnp.concatenate([high, low], axis=1), right, preferred_element_type=jnp.float32
        )
        left = (both[:, : 2 * size] + both[:, 2 * size :]).reshape(pairs, size, 2 * size)
        left = left * weights[:, cols].reshape(pairs, 1, 2 * size)
        left_high, left_low = split(left)
        left_ref[:, :size, cols] = left_high
        left_ref[:, size:, cols] = left_low


def add_products(first, cat_ref, left_ref, acc_ref):
    for s in range(acc_ref.shape[0]):
        total = jnp.where(first, 0.0, acc_ref[s])
        for c in range(cat_ref.shape[0]):
            total += lax.dot_general(
                left_ref[c, s], cat_ref[c, s], NT, preferred_element_type=jnp.float32
            )
        acc_ref[s] = total


def cross_chunk(atoms, own_ref, payload_ref, cat_ref, full_ref):
    columns = own_ref.shape[1]
    pairs, rows2, unused = cat_ref.shape
    size = rows2 // 2
    for k in range(2 * CHUNK):
        n, c = k // 2, k % 2
        full_ref[k * size : (k + 1) * size, :] = lax.dot_general(
            payload_ref[n, c * size : (c + 1) * size, :],
            column_table(atoms[k : k + 1, :], columns), NT, preferred_element_type=jnp.float32,
        ).astype(jnp.bfloat16)
    cross = lax.dot_general(own_ref[...], full_ref[...], NT, preferred_element_type=jnp.float32)
    high, low = split(cross)
    cat_ref[:, :size, :] = high.reshape(pairs, size, -1)
    cat_ref[:, size:, :] = low.reshape(pairs, size, -1)


def coupled_of(acc):
    size = acc.shape[0] // 2
    rows = acc[:size] + acc[size:]
    return rows[:, :size] + rows[:, size:]


def first_kernel(
    half_ref, request_ref, wanted_ref, table_ref, own_ref, payload_ref, weight_ref, position_ref,
    current_ref, integrals_ref, denominator_ref, cat_ref, new_ref, send_hbm, full_ref, left_ref,
    acc_ref, info_ref, send_ref, even_ref, odd_ref, sem_ref,
):
    pairs, size, unused = denominator_ref.shape
    width = payload_ref.shape[2]
    chunks = cat_ref.shape[0]
    near = wanted_ref.shape[0] // 2
    half = half_ref[0]
    step = pl.program_id(0)
    count = table_ref.shape[2] - size - request_ref.shape[1]
    entries = CHUNK * chunks
    lanes = table_ref.shape[2]
    for k in range(2 * entries):
        source = source_of(step * entries + k // 2, half, near)
        row = request_ref[0, source * 2 + k % 2]
        info_ref[k : k + 1, :lanes] = table_ref[source, pl.ds(row, 1), :lanes]
    atoms = atoms_of_columns(info_ref[:, size : size + count], width)
    scales = info_ref[:, : 2 * size].astype(jnp.float32)
    moved = pltpu.roll(scales, size, 1)
    left_lanes = lax.broadcasted_iota(jnp.int32, (1, 2 * size), 1) < size

    for c in range(chunks):
        blocks = payload_ref.at[pl.ds(c * CHUNK, CHUNK)]
        cross_chunk(
            atoms[c * 2 * CHUNK : (c + 1) * 2 * CHUNK], own_ref, blocks, cat_ref.at[c],
            full_ref.at[c],
        )
        start = step * entries + c * CHUNK
        weights = slot_weights(half, near, start, weight_ref, position_ref, size)

        def amps(j, c=c, blocks=blocks):
            k = 2 * (c * CHUNK + j)
            eighths = jnp.where(left_lanes, scales[k : k + 1, :], moved[k + 1 : k + 2, :])
            logs = blocks[j, 2 * size :, :].astype(jnp.float32)
            return block_of_logs(logs, eighths)

        half_products(weights, amps, cat_ref.at[c], left_ref.at[c])
    add_products(step == 0, cat_ref, left_ref, acc_ref)

    @pl.when(step == pl.num_programs(0) - 1)
    def finish():
        for s in range(pairs):
            rows = slice(s * size, (s + 1) * size)
            current, denominator = current_ref[rows, :], denominator_ref[s]
            residual = integrals_ref[rows, :] + denominator * current - coupled_of(acc_ref[s])
            new = current - residual / denominator
            new_ref[rows, :] = new
            store_codes(new, even_ref, odd_ref, s)

        def pack(d, carry):
            send_ref[d] = even_ref[wanted_ref[d, 0]] + odd_ref[wanted_ref[d, 1]]
            return carry

        lax.fori_loop(0, send_ref.shape[0], pack, 0)
        copy = pltpu.make_async_copy(send_ref, send_hbm, sem_ref.at[0])
        copy.start()
        copy.wait()


def second_kernel(
    half_ref, cat_ref, weight_ref, position_ref, amp_ref, current_ref, integrals_ref,
    denominator_ref, new_ref, residual_ref, left_ref, acc_ref, new_rows_ref, residual_rows_ref,
):
    pairs, size, unused = denominator_ref.shape
    step = pl.program_id(0)
    half = half_ref[0]
    near = amp_ref.shape[0] // 2
    chunks = cat_ref.shape[0]
    for c in range(chunks):
        start = (step * chunks + c) * CHUNK
        weights = slot_weights(half, near, start, weight_ref, position_ref, size)
        half_products(
            weights, lambda j: block_of_codes(amp_ref[source_of(start + j, half, near)]),
            cat_ref.at[c], left_ref.at[c],
        )
    add_products(step == 0, cat_ref, left_ref, acc_ref)

    @pl.when(step == pl.num_programs(0) - 1)
    def finish():
        for s in range(pairs):
            rows = slice(s * size, (s + 1) * size)
            current, denominator = current_ref[rows, :], denominator_ref[s]
            residual = integrals_ref[rows, :] + denominator * current - coupled_of(acc_ref[s])
            residual_rows_ref[rows, :] = residual
            new_rows_ref[rows, :] = current - residual / denominator
        for rows_ref, out_ref in ((residual_rows_ref, residual_ref), (new_rows_ref, new_ref)):
            for a in range(0, size, 2):
                out_ref[:, a * size : (a + 2) * size] = jnp.concatenate(
                    [rows_ref[pl.ds(a + i, pairs, stride=size), :] for i in range(2)], axis=1
                )


def smem():
    return pl.BlockSpec(memory_space=pltpu.SMEM)


def vmem():
    return pl.BlockSpec(memory_space=pltpu.VMEM)


def hbm():
    return pl.BlockSpec(memory_space=pltpu.HBM)


def in_hbm(*arrays):
    return [pltpu.with_memory_space_constraint(array, pltpu.HBM) for array in arrays]


def params():
    return pltpu.CompilerParams(
        dimension_semantics=("arbitrary",), vmem_limit_bytes=VMEM_LIMIT
    )


def limit():
    return pltpu.CompilerParams(vmem_limit_bytes=VMEM_LIMIT)


def prepare(pnos, domains, amplitudes, integrals):
    pairs, size, width = pnos.shape
    own = (pairs * size, ATOMS * (width // domains.shape[1]))
    block = (pairs * size, size)
    return pl.pallas_call(
        prepare_kernel,
        in_specs=[vmem()] * 4,
        out_specs=[vmem()] * 3,
        out_shape=[
            jax.ShapeDtypeStruct(own, jnp.bfloat16), jax.ShapeDtypeStruct(block, jnp.float32),
            jax.ShapeDtypeStruct(block, jnp.float32),
        ],
        scratch_shapes=[pltpu.VMEM((pairs, width), jnp.float32)],
        compiler_params=limit(),
        name="prepare",
    )(pnos, domains, amplitudes, integrals)


def encode(amplitudes, domains, request, size):
    pairs = amplitudes.shape[0]
    lanes = size + domains.shape[1] + request.shape[1]
    return pl.pallas_call(
        encode_kernel,
        in_specs=[hbm()] * 3,
        out_specs=[vmem()] * 2,
        out_shape=[
            jax.ShapeDtypeStruct((pairs, size // 2, 2 * size), jnp.bfloat16),
            jax.ShapeDtypeStruct((pairs, lanes), jnp.int32),
        ],
        scratch_shapes=[
            pltpu.VMEM(amplitudes.shape, jnp.float32), pltpu.VMEM(domains.shape, jnp.int32),
            pltpu.VMEM(request.shape, jnp.int32), pltpu.VMEM((pairs * size, size), jnp.float32),
            pltpu.SemaphoreType.DMA((3,)),
        ],
        compiler_params=limit(),
        name="encode",
    )(*in_hbm(amplitudes, domains, request))


def pack_payload(here, there, pnos, logs, far_pnos, far_logs):
    unused, size, width = pnos.shape
    rows = 2 * size + logs.shape[1]
    return pl.pallas_call(
        pack_kernel,
        in_specs=[smem(), smem()] + [vmem()] * 4,
        out_specs=vmem(),
        out_shape=jax.ShapeDtypeStruct((here.shape[0], 2, rows, width), jnp.bfloat16),
        compiler_params=limit(),
        name="pack_payload",
    )(here, there, pnos, logs, far_pnos, far_logs)


def sweep_shapes(entries, pairs, size):
    chunks = entries // CHUNK if entries <= ONE_STEP else 1
    cat = (entries // CHUNK, pairs, 2 * size, 2 * CHUNK * size)
    held = (chunks,) + cat[1:]
    scratch = [
        pltpu.VMEM(held, jnp.bfloat16), pltpu.VMEM(held, jnp.bfloat16),
        pltpu.VMEM((pairs, 2 * size, 2 * size), jnp.float32),
    ]
    return cat[0] // chunks, chunks, cat, scratch


def cat_spec(steps, chunks, cat):
    if steps == 1:
        return vmem()
    return pl.BlockSpec((chunks,) + cat[1:], lambda i: (i, 0, 0, 0))


def first_sweep(
    half, request, wanted, table, own, payload, weight, position, current, integrals, denominator
):
    pairs, size, unused = denominator.shape
    entries, rows, width = payload.shape
    steps, chunks, cat, (cats, lefts, acc) = sweep_shapes(entries, pairs, size)
    block = (CHUNK * chunks, rows, width)
    blocks = vmem() if steps == 1 else pl.BlockSpec(block, lambda i: (i, 0, 0))
    kept = cat_spec(steps, chunks, cat)
    parts = (pairs, size + CODE_ROWS, 2 * size)
    send = (entries,) + parts[1:]
    return pl.pallas_call(
        first_kernel,
        grid=(steps,),
        in_specs=[smem()] * 3 + [vmem(), vmem(), blocks] + [vmem()] * 5,
        out_specs=[kept, vmem(), hbm()],
        out_shape=[
            jax.ShapeDtypeStruct(cat, jnp.bfloat16),
            jax.ShapeDtypeStruct(current.shape, jnp.float32),
            pltpu.HBM(send, jnp.int16),
        ],
        scratch_shapes=[
            pltpu.VMEM((chunks, cat[3], own.shape[1]), jnp.bfloat16),
            lefts,
            acc,
            pltpu.VMEM((2 * CHUNK * chunks, max(table.shape[2], 2 * size)), jnp.int32),
            pltpu.VMEM(send, jnp.int16),
            pltpu.VMEM(parts, jnp.int16),
            pltpu.VMEM(parts, jnp.int16),
            pltpu.SemaphoreType.DMA((1,)),
        ],
        compiler_params=params(),
        name="first_sweep",
    )(
        half, request, wanted, table, own, payload, weight, position, current, integrals,
        denominator,
    )


def second_sweep(half, cat, weight, position, amp, current, integrals, denominator):
    pairs, size, unused = denominator.shape
    steps, chunks, shape, scratch = sweep_shapes(amp.shape[0], pairs, size)
    flat = (pairs, size * size)
    return pl.pallas_call(
        second_kernel,
        grid=(steps,),
        in_specs=[smem(), cat_spec(steps, chunks, shape)] + [vmem()] * 6,
        out_specs=[vmem(), vmem()],
        out_shape=[jax.ShapeDtypeStruct(flat, jnp.float32)] * 2,
        scratch_shapes=scratch[1:] + [
            pltpu.VMEM(current.shape, jnp.float32),
            pltpu.VMEM(current.shape, jnp.float32),
        ],
        compiler_params=params(),
        name="second_sweep",
    )(
        half, cat, weight, position, amp, current, integrals, denominator
    )


def on_device(
    amplitudes, integrals, virtual, occupied, coupling, degree, position, request, pnos, domains
):
    pairs = amplitudes.shape[0]
    size = virtual.shape[1]
    depth = coupling.shape[1]
    slots = request.shape[1]
    entries = slots // 2
    near = entries // 2
    half = lax.axis_index("half").astype(jnp.int32)
    mine = lax.axis_index("near").astype(jnp.int32)
    swap = [(0, 1), (1, 0)]
    both = ("half", "near")

    far_pnos = lax.ppermute(pnos, "half", swap)
    logs, table = encode(amplitudes, domains, request, size)
    far_logs = lax.ppermute(logs, "half", swap)

    def gather(row):
        rows = jnp.broadcast_to(row[None], (entries,) + row.shape)
        return lax.all_to_all(rows, both, split_axis=0, concat_axis=0, tiled=True)

    def nothing(row):
        return jnp.zeros((entries,) + row.shape, jnp.int32)

    table = lax.cond(degree[0] > 0, gather, nothing, table)
    column = table.shape[2] - slots + 2 * mine
    wanted = lax.dynamic_slice(
        table, (0, 0, column + half * 2 * near), (entries, 1, 2)
    ).reshape(entries, 2)
    here = lax.dynamic_slice(wanted, (half * near, 0), (near, 2))
    there = lax.dynamic_slice(
        table, (half * near, 0, column + (1 - half) * 2 * near), (near, 1, 2)
    ).reshape(near, 2)

    payload = pack_payload(here, there, pnos, logs, far_pnos, far_logs)
    payload = lax.all_to_all(payload, "near", split_axis=0, concat_axis=0, tiled=True)
    payload = payload.reshape((entries,) + payload.shape[2:])

    live = jnp.arange(depth, dtype=jnp.int32)[None, :] < degree[:, None]
    weight = jnp.where(live, coupling, jnp.zeros_like(coupling))
    denominator = virtual[:, :, None] + virtual[:, None, :] - occupied[:, None, None]
    own, current, integrals = prepare(pnos, domains, amplitudes, integrals)
    half = half.reshape(1)
    cat, current, amp = first_sweep(
        half, request, wanted, table, own, payload, weight, position, current, integrals,
        denominator,
    )
    amp = lax.all_to_all(amp, both, split_axis=0, concat_axis=0, tiled=True)
    new, residual = second_sweep(
        half, cat, weight, position, amp, current, integrals, denominator
    )
    return new, residual


def solution(mesh):
    count = mesh.shape["pair"]
    devices = mesh.devices.reshape(mesh.shape["frag"], 2, count // 2)
    split_mesh = Mesh(devices, ("frag", "half", "near"))
    rows = ("frag", "half", "near")
    return jax.shard_map(
        on_device,
        mesh=split_mesh,
        in_specs=(
            P(rows, None), P(rows, None), P(rows, None), P(rows), P(rows, None),
            P(rows), P(rows, None), P(rows, None), P(rows, None, None), P(rows, None),
        ),
        out_specs=(P(rows, None), P(rows, None)),
        check_vma=False,
    )
```

```python
import jax
import jax.numpy as jnp
from jax import lax
from jax.experimental import pallas as pl
from jax.experimental.pallas import tpu as pltpu
from jax.sharding import Mesh, PartitionSpec as P

ATOMS = 32
CHUNK = 4
ONE_STEP = 16
LOG_TOP = 125.0
CODE_TOP = 32767.0
CODE_ROWS = 16
SMALLEST = 2.0**-100
VMEM_LIMIT = 32 * 1024 * 1024
NT = (((1,), (1,)), ((), ()))


def split(value):
    high = value.astype(jnp.bfloat16)
    low = (value - high.astype(jnp.float32)).astype(jnp.bfloat16)
    return high, low


def scale_of(eighths):
    return jnp.exp2(eighths * 0.125)


def eighths_of(value):
    top = jnp.maximum(jnp.max(jnp.abs(value), axis=0, keepdims=True), SMALLEST)
    return jnp.ceil(jnp.log2(top) * 8.0)


def store_codes(value, even_ref, odd_ref, p):
    size = value.shape[0]
    eighths = eighths_of(value)
    codes = jnp.clip(jnp.round(value * (CODE_TOP / scale_of(eighths))), -CODE_TOP, CODE_TOP)
    rows = jnp.concatenate([codes, jnp.broadcast_to(eighths, (CODE_ROWS, size))], axis=0)
    blank = jnp.zeros_like(rows)
    for ref, parts in ((even_ref, [rows, blank]), (odd_ref, [blank, rows])):
        ref[p] = jnp.concatenate(parts, axis=1).astype(jnp.int32).astype(jnp.int16)


def block_of_codes(codes):
    rows = codes.astype(jnp.int32).astype(jnp.float32)
    size = rows.shape[0] - CODE_ROWS
    return rows[:size, :] * (scale_of(rows[size : size + 1, :]) * (1.0 / CODE_TOP))


def log_code(value, eighths):
    power = jnp.clip(value * (LOG_TOP / scale_of(eighths)), -LOG_TOP, LOG_TOP)
    return jnp.exp2(power)


def block_of_logs(first, second, eighths):
    rows, lanes = first.shape[0], eighths.shape[1]
    size = lanes // 2
    left = lax.broadcasted_iota(jnp.int32, (rows, lanes), 1) < size
    quarters = []
    for start in range(0, 2 * lanes, lanes):
        a, b = first[:, start : start + lanes], second[:, start : start + lanes]
        quarters.append(jnp.where(left, a, pltpu.roll(b, size, 1)))
        quarters.append(jnp.where(left, pltpu.roll(a, size, 1), b))
    both = jnp.concatenate(quarters, axis=0)
    return jnp.log2(both) * (scale_of(eighths) * (1.0 / LOG_TOP))


def to_blocks(flat_ref, rows_ref, size):
    pairs = flat_ref.shape[0]
    for a in range(0, size, 2):
        both = flat_ref[:, a * size : (a + 2) * size]
        rows_ref[pl.ds(a, pairs, stride=size), :] = both[:, :size]
        rows_ref[pl.ds(a + 1, pairs, stride=size), :] = both[:, size:]


def atoms_of_columns(domains, width):
    count = domains.shape[1]
    entry = lax.broadcasted_iota(jnp.int32, (count, width), 0)
    column = lax.broadcasted_iota(jnp.int32, (count, width), 1)
    spread = (entry == column // (width // count)).astype(jnp.float32).astype(jnp.bfloat16)
    atoms = domains.astype(jnp.float32).astype(jnp.bfloat16)
    return jnp.dot(atoms, spread, preferred_element_type=jnp.float32)


def column_table(atoms, columns):
    width = atoms.shape[1]
    per_atom = columns // ATOMS
    row = lax.broadcasted_iota(jnp.int32, (columns, width), 0).astype(jnp.int16)
    column = lax.broadcasted_iota(jnp.int32, (1, width), 1)
    ids = (atoms.astype(jnp.int32) * per_atom + column % per_atom).astype(jnp.int16)
    return jnp.where(row == ids, jnp.ones((), jnp.bfloat16), jnp.zeros((), jnp.bfloat16))


def prepare_kernel(
    half_ref, request_ref, table_ref, pnos_ref, domains_ref, amp_ref, integrals_ref, weight_ref,
    position_ref, own_ref, current_ref, blocks_ref, atoms_ref, scales_ref, weights_ref, mask_ref,
    own_atoms_ref, info_ref,
):
    pairs, size, width = pnos_ref.shape
    columns = own_ref.shape[1]
    entries = scales_ref.shape[0]
    half = half_ref[0]
    to_blocks(amp_ref, current_ref, size)
    to_blocks(integrals_ref, blocks_ref, size)
    own_atoms_ref[...] = atoms_of_columns(domains_ref[...], width)
    for p in range(pairs):
        own_ref[p * size : (p + 1) * size, :] = lax.dot_general(
            pnos_ref[p], column_table(own_atoms_ref[p : p + 1, :], columns), NT,
            preferred_element_type=jnp.float32,
        ).astype(jnp.bfloat16)

    count = domains_ref.shape[1]
    lanes = table_ref.shape[2]
    for k in range(2 * entries):
        source = source_of(k // 2, half, entries // 2)
        row = request_ref[0, source * 2 + k % 2]
        info_ref[k : k + 1, :lanes] = table_ref[source, pl.ds(row, 1), :]
    atoms_ref[...] = atoms_of_columns(info_ref[:, size : size + count], width)
    scales = info_ref[:, : 2 * size].astype(jnp.float32)
    moved = pltpu.roll(scales, size, 1)
    left_lanes = lax.broadcasted_iota(jnp.int32, (1, 2 * size), 1) < size
    for e in range(entries):
        scales_ref[e : e + 1, :] = jnp.where(
            left_lanes, scales[2 * e : 2 * e + 1, :], moved[2 * e + 1 : 2 * e + 2, :]
        )
    for c in range(weights_ref.shape[0]):
        weights_ref[c] = slot_weights(
            half, entries // 2, c * CHUNK, weight_ref, position_ref, size
        )
    mask_ref[...] = jnp.full_like(mask_ref, half)


def encode_kernel(
    pnos_hbm, amp_hbm, domains_hbm, request_hbm, pnos_ref, logs_ref, table_ref, amp_ref,
    domains_ref, request_ref, rows_ref, sem_ref,
):
    pairs, size, unused = pnos_hbm.shape
    quarter = logs_ref.shape[1]
    copies = [
        pltpu.make_async_copy(amp_hbm, amp_ref, sem_ref.at[0]),
        pltpu.make_async_copy(domains_hbm, domains_ref, sem_ref.at[1]),
        pltpu.make_async_copy(request_hbm, request_ref, sem_ref.at[2]),
        pltpu.make_async_copy(pnos_hbm, pnos_ref, sem_ref.at[3]),
    ]
    for copy in copies:
        copy.start()
    for copy in copies[:3]:
        copy.wait()
    to_blocks(amp_ref, rows_ref, size)
    scales = []
    for p in range(pairs):
        block = rows_ref[p * size : (p + 1) * size, :]
        eighths = eighths_of(block)
        logs = log_code(block, eighths)
        logs_ref[p] = jnp.concatenate(
            [logs[q : q + quarter, :] for q in range(0, size, quarter)], axis=1
        ).astype(jnp.bfloat16)
        scales.append(eighths)
    scales = jnp.concatenate(scales, axis=0).astype(jnp.int32)
    count = domains_ref.shape[1]
    slots = request_ref.shape[1]
    table_ref[:, :size] = scales
    table_ref[:, size : size + count] = domains_ref[...]
    table_ref[:, size + count :] = jnp.broadcast_to(request_ref[...], (pairs, slots))
    copies[3].wait()


def pack_kernel(
    here_ref, there_ref, pnos_ref, logs_ref, far_pnos_ref, far_logs_ref, out_hbm, sem_ref
):
    unused, size, width = pnos_ref.shape
    quarter = logs_ref.shape[1]

    def pack(n, carry):
        parts = ((here_ref, pnos_ref, logs_ref), (there_ref, far_pnos_ref, far_logs_ref))
        for part, (wanted_ref, blocks_ref, codes_ref) in enumerate(parts):
            for c in range(2):
                pair = wanted_ref[n, c]
                to = out_hbm.at[n, part, c]
                pltpu.make_async_copy(
                    blocks_ref.at[pair], to.at[pl.ds(0, size)], sem_ref.at[0]
                ).start()
                pltpu.make_async_copy(
                    codes_ref.at[pair], to.at[pl.ds(size, quarter)], sem_ref.at[0]
                ).start()
        return carry

    lax.fori_loop(0, out_hbm.shape[0], pack, 0)
    pltpu.make_async_copy(out_hbm, out_hbm, sem_ref.at[0]).wait()


def source_of(entry, half, near):
    return (entry % 2 + half) % 2 * near + entry // 2


def slot_weights(half, near, start, weight_ref, position_ref, size):
    slot = lax.broadcasted_iota(jnp.int32, (1, 2 * CHUNK * size), 1) // size
    source = source_of(start + slot // 2, half, near)
    named = source * 2 + slot % 2
    total = jnp.zeros((weight_ref.shape[0], named.shape[1]), jnp.float32)
    for c in range(weight_ref.shape[1]):
        hit = position_ref[:, c : c + 1] == named
        total += jnp.where(hit, weight_ref[:, c : c + 1], 0.0)
    return total


def half_products(weights, amps, cat_ref, left_ref):
    pairs, rows2, lanes = cat_ref.shape
    size = rows2 // 2
    group = lax.broadcasted_iota(jnp.int32, (size, 4 * size), 1) // size
    even = (group % 2 == 0).astype(jnp.float32).astype(jnp.bfloat16)
    odd = (group % 2 == 1).astype(jnp.float32).astype(jnp.bfloat16)
    for j in range(CHUNK):
        cols = slice(j * 2 * size, (j + 1) * 2 * size)
        amp = jnp.concatenate(split(amps(j)), axis=1)
        first, second = amp * even, amp * odd
        right = jnp.concatenate([first, second, first, second], axis=0)
        high = cat_ref[:, :size, cols].reshape(pairs * size, 2 * size)
        low = cat_ref[:, size:, cols].reshape(pairs * size, 2 * size)
        both = jnp.dot(
            jnp.concatenate([high, low], axis=1), right, preferred_element_type=jnp.float32
        )
        left = (both[:, : 2 * size] + both[:, 2 * size :]).reshape(pairs, size, 2 * size)
        left = left * weights[:, cols].reshape(pairs, 1, 2 * size)
        left_high, left_low = split(left)
        left_ref[:, :size, cols] = left_high
        left_ref[:, size:, cols] = left_low


def add_products(first, cat_ref, left_ref, acc_ref):
    for s in range(acc_ref.shape[0]):
        total = jnp.where(first, 0.0, acc_ref[s])
        for c in range(cat_ref.shape[0]):
            total += lax.dot_general(
                left_ref[c, s], cat_ref[c, s], NT, preferred_element_type=jnp.float32
            )
        acc_ref[s] = total


def cross_chunk(atoms, own_ref, payload_ref, cat_ref, full_ref):
    columns = own_ref.shape[1]
    pairs, rows2, unused = cat_ref.shape
    size = rows2 // 2
    for k in range(2 * CHUNK):
        n, c = k // 2, k % 2
        full_ref[k * size : (k + 1) * size, :] = lax.dot_general(
            payload_ref[n, c, :size, :],
            column_table(atoms[k : k + 1, :], columns), NT, preferred_element_type=jnp.float32,
        ).astype(jnp.bfloat16)
    cross = lax.dot_general(own_ref[...], full_ref[...], NT, preferred_element_type=jnp.float32)
    high, low = split(cross)
    cat_ref[:, :size, :] = high.reshape(pairs, size, -1)
    cat_ref[:, size:, :] = low.reshape(pairs, size, -1)


def coupled_of(acc):
    size = acc.shape[0] // 2
    rows = acc[:size] + acc[size:]
    return rows[:, :size] + rows[:, size:]


def first_kernel(
    wanted_hbm, own_ref, payload_ref, atoms_ref, scales_ref, weights_ref, current_ref,
    integrals_ref, denominator_ref, cat_ref, new_ref, send_hbm, full_ref, left_ref, acc_ref,
    send_ref, even_ref, odd_ref, wanted_ref, sem_ref,
):
    pairs, size, unused = denominator_ref.shape
    chunks = cat_ref.shape[0]
    step = pl.program_id(0)
    wanted_copy = pltpu.make_async_copy(wanted_hbm, wanted_ref, sem_ref.at[0])

    @pl.when(step == 0)
    def fetch():
        wanted_copy.start()

    for c in range(chunks):
        blocks = payload_ref.at[pl.ds(c * CHUNK, CHUNK)]
        chunk = step * chunks + c
        atoms = atoms_ref[pl.ds(chunk * 2 * CHUNK, 2 * CHUNK), :]
        cross_chunk(atoms, own_ref, blocks, cat_ref.at[c], full_ref.at[c])

        def amps(j, chunk=chunk, blocks=blocks):
            eighths = scales_ref[pl.ds(chunk * CHUNK + j, 1), :]
            logs = [blocks[j, i, size:, :].astype(jnp.float32) for i in range(2)]
            return block_of_logs(*logs, eighths)

        half_products(weights_ref[chunk], amps, cat_ref.at[c], left_ref.at[c])
    add_products(step == 0, cat_ref, left_ref, acc_ref)

    @pl.when(step == pl.num_programs(0) - 1)
    def finish():
        for s in range(pairs):
            rows = slice(s * size, (s + 1) * size)
            current, denominator = current_ref[rows, :], denominator_ref[s]
            residual = integrals_ref[rows, :] + denominator * current - coupled_of(acc_ref[s])
            new = current - residual / denominator
            new_ref[rows, :] = new
            store_codes(new, even_ref, odd_ref, s)

        wanted_copy.wait()

        def pack(d, carry):
            send_ref[d] = even_ref[wanted_ref[d, 0]] + odd_ref[wanted_ref[d, 1]]
            return carry

        lax.fori_loop(0, send_ref.shape[0], pack, 0)
        copy = pltpu.make_async_copy(send_ref, send_hbm, sem_ref.at[0])
        copy.start()
        copy.wait()


def second_kernel(
    mask_ref, cat_ref, weights_ref, amp_ref, current_ref, integrals_ref, denominator_ref,
    new_ref, residual_ref, left_ref, acc_ref, new_rows_ref, residual_rows_ref,
):
    pairs, size, unused = denominator_ref.shape
    step = pl.program_id(0)
    near = amp_ref.shape[0] // 2
    chunks = cat_ref.shape[0]
    upper = mask_ref[:1, :] > 0
    for c in range(chunks):
        chunk = step * chunks + c

        def amps(j, chunk=chunk):
            entry = chunk * CHUNK + j
            low = block_of_codes(amp_ref[entry // 2])
            high = block_of_codes(amp_ref[near + entry // 2])
            return jnp.where(upper, low, high) if j % 2 else jnp.where(upper, high, low)

        half_products(weights_ref[chunk], amps, cat_ref.at[c], left_ref.at[c])
    add_products(step == 0, cat_ref, left_ref, acc_ref)

    @pl.when(step == pl.num_programs(0) - 1)
    def finish():
        for s in range(pairs):
            rows = slice(s * size, (s + 1) * size)
            current, denominator = current_ref[rows, :], denominator_ref[s]
            residual = integrals_ref[rows, :] + denominator * current - coupled_of(acc_ref[s])
            residual_rows_ref[rows, :] = residual
            new_rows_ref[rows, :] = current - residual / denominator
        for rows_ref, out_ref in ((residual_rows_ref, residual_ref), (new_rows_ref, new_ref)):
            for a in range(0, size, 2):
                out_ref[:, a * size : (a + 2) * size] = jnp.concatenate(
                    [rows_ref[pl.ds(a + i, pairs, stride=size), :] for i in range(2)], axis=1
                )


def smem():
    return pl.BlockSpec(memory_space=pltpu.SMEM)


def vmem():
    return pl.BlockSpec(memory_space=pltpu.VMEM)


def hbm():
    return pl.BlockSpec(memory_space=pltpu.HBM)


def in_hbm(*arrays):
    return [pltpu.with_memory_space_constraint(array, pltpu.HBM) for array in arrays]


def params():
    return pltpu.CompilerParams(
        dimension_semantics=("arbitrary",), vmem_limit_bytes=VMEM_LIMIT
    )


def limit():
    return pltpu.CompilerParams(vmem_limit_bytes=VMEM_LIMIT)


def prepare(half, request, table, pnos, domains, amplitudes, integrals, weight, position):
    pairs, size, width = pnos.shape
    entries = request.shape[1] // 2
    own = (pairs * size, ATOMS * (width // domains.shape[1]))
    block = (pairs * size, size)
    out = (
        (own, jnp.bfloat16), (block, jnp.float32), (block, jnp.float32),
        ((2 * entries, width), jnp.float32), ((entries, 2 * size), jnp.float32),
        ((entries // CHUNK, pairs, 2 * CHUNK * size), jnp.float32), ((8, 2 * size), jnp.int32),
    )
    return pl.pallas_call(
        prepare_kernel,
        in_specs=[smem()] * 2 + [vmem()] * 7,
        out_specs=[vmem()] * len(out),
        out_shape=[jax.ShapeDtypeStruct(shape, dtype) for shape, dtype in out],
        scratch_shapes=[
            pltpu.VMEM((pairs, width), jnp.float32),
            pltpu.VMEM((2 * entries, max(table.shape[2], 2 * size)), jnp.int32),
        ],
        compiler_params=limit(),
        name="prepare",
    )(half, request, table, pnos, domains, amplitudes, integrals, weight, position)


def encode(pnos, amplitudes, domains, request):
    pairs, size, width = pnos.shape
    quarter = size * size // width
    lanes = size + domains.shape[1] + request.shape[1]
    return pl.pallas_call(
        encode_kernel,
        in_specs=[hbm()] * 4,
        out_specs=[vmem()] * 3,
        out_shape=[
            jax.ShapeDtypeStruct(pnos.shape, jnp.bfloat16),
            jax.ShapeDtypeStruct((pairs, quarter, width), jnp.bfloat16),
            jax.ShapeDtypeStruct((pairs, lanes), jnp.int32),
        ],
        scratch_shapes=[
            pltpu.VMEM(amplitudes.shape, jnp.float32), pltpu.VMEM(domains.shape, jnp.int32),
            pltpu.VMEM(request.shape, jnp.int32), pltpu.VMEM((pairs * size, size), jnp.float32),
            pltpu.SemaphoreType.DMA((4,)),
        ],
        compiler_params=limit(),
        name="encode",
    )(*in_hbm(pnos, amplitudes, domains, request))


def pack_payload(here, there, pnos, logs, far_pnos, far_logs):
    unused, size, width = pnos.shape
    out = (here.shape[0], 2, 2, size + logs.shape[1], width)
    return pl.pallas_call(
        pack_kernel,
        in_specs=[smem(), smem()] + [vmem()] * 4,
        out_specs=hbm(),
        out_shape=pltpu.HBM(out, pnos.dtype),
        scratch_shapes=[pltpu.SemaphoreType.DMA((1,))],
        compiler_params=limit(),
        name="pack_payload",
    )(here, there, pnos, logs, far_pnos, far_logs)


def sweep_shapes(entries, pairs, size):
    chunks = entries // CHUNK if entries <= ONE_STEP else 1
    cat = (entries // CHUNK, pairs, 2 * size, 2 * CHUNK * size)
    held = (chunks,) + cat[1:]
    scratch = [
        pltpu.VMEM(held, jnp.bfloat16), pltpu.VMEM(held, jnp.bfloat16),
        pltpu.VMEM((pairs, 2 * size, 2 * size), jnp.float32),
    ]
    return cat[0] // chunks, chunks, cat, scratch


def cat_spec(steps, chunks, cat):
    if steps == 1:
        return vmem()
    return pl.BlockSpec((chunks,) + cat[1:], lambda i: (i, 0, 0, 0))


def first_sweep(
    wanted, own, payload, atoms, scales, weights, current, integrals, denominator
):
    pairs, size, unused = denominator.shape
    entries = payload.shape[0]
    steps, chunks, cat, (cats, lefts, acc) = sweep_shapes(entries, pairs, size)
    block = (CHUNK * chunks,) + payload.shape[1:]
    blocks = vmem() if steps == 1 else pl.BlockSpec(block, lambda i: (i, 0, 0, 0))
    kept = cat_spec(steps, chunks, cat)
    parts = (pairs, size + CODE_ROWS, 2 * size)
    send = (entries,) + parts[1:]
    return pl.pallas_call(
        first_kernel,
        grid=(steps,),
        in_specs=[hbm(), vmem(), blocks] + [vmem()] * 6,
        out_specs=[kept, vmem(), hbm()],
        out_shape=[
            jax.ShapeDtypeStruct(cat, jnp.bfloat16),
            jax.ShapeDtypeStruct(current.shape, jnp.float32),
            pltpu.HBM(send, jnp.int16),
        ],
        scratch_shapes=[
            pltpu.VMEM((chunks, cat[3], own.shape[1]), jnp.bfloat16),
            lefts,
            acc,
            pltpu.VMEM(send, jnp.int16),
            pltpu.VMEM(parts, jnp.int16),
            pltpu.VMEM(parts, jnp.int16),
            pltpu.SMEM(wanted.shape, jnp.int32),
            pltpu.SemaphoreType.DMA((1,)),
        ],
        compiler_params=params(),
        name="first_sweep",
    )(
        *in_hbm(wanted), own, payload, atoms, scales, weights, current, integrals, denominator
    )


def second_sweep(mask, cat, weights, amp, current, integrals, denominator):
    pairs, size, unused = denominator.shape
    steps, chunks, shape, scratch = sweep_shapes(amp.shape[0], pairs, size)
    flat = (pairs, size * size)
    return pl.pallas_call(
        second_kernel,
        grid=(steps,),
        in_specs=[vmem(), cat_spec(steps, chunks, shape)] + [vmem()] * 5,
        out_specs=[vmem(), vmem()],
        out_shape=[jax.ShapeDtypeStruct(flat, jnp.float32)] * 2,
        scratch_shapes=scratch[1:] + [
            pltpu.VMEM(current.shape, jnp.float32),
            pltpu.VMEM(current.shape, jnp.float32),
        ],
        compiler_params=params(),
        name="second_sweep",
    )(
        mask, cat, weights, amp, current, integrals, denominator
    )


def on_device(
    amplitudes, integrals, virtual, occupied, coupling, degree, position, request, pnos, domains
):
    pairs = amplitudes.shape[0]
    size = virtual.shape[1]
    depth = coupling.shape[1]
    slots = request.shape[1]
    entries = slots // 2
    near = entries // 2
    half = lax.axis_index("half").astype(jnp.int32)
    mine = lax.axis_index("near").astype(jnp.int32)
    swap = [(0, 1), (1, 0)]
    both = ("half", "near")

    far_pnos = lax.ppermute(pnos, "half", swap)
    near_pnos, logs, table = encode(pnos, amplitudes, domains, request)
    far_logs = lax.ppermute(logs, "half", swap)

    def gather(row):
        rows = jnp.broadcast_to(row[None], (entries,) + row.shape)
        return lax.all_to_all(rows, both, split_axis=0, concat_axis=0, tiled=True)

    def nothing(row):
        return jnp.zeros((entries,) + row.shape, jnp.int32)

    table = lax.cond(degree[0] > 0, gather, nothing, table)
    column = table.shape[2] - slots + 2 * mine
    wanted = lax.dynamic_slice(
        table, (0, 0, column + half * 2 * near), (entries, 1, 2)
    ).reshape(entries, 2)
    here = lax.dynamic_slice(wanted, (half * near, 0), (near, 2))
    there = lax.dynamic_slice(
        table, (half * near, 0, column + (1 - half) * 2 * near), (near, 1, 2)
    ).reshape(near, 2)

    payload = pack_payload(here, there, near_pnos, logs, far_pnos, far_logs)
    payload = lax.all_to_all(payload, "near", split_axis=0, concat_axis=0, tiled=True)
    payload = payload.reshape((entries,) + payload.shape[2:])

    live = jnp.arange(depth, dtype=jnp.int32)[None, :] < degree[:, None]
    weight = jnp.where(live, coupling, jnp.zeros_like(coupling))
    denominator = virtual[:, :, None] + virtual[:, None, :] - occupied[:, None, None]
    own, current, integrals, atoms, scales, weights, mask = prepare(
        half.reshape(1), request, table, pnos, domains, amplitudes, integrals, weight, position
    )
    cat, current, amp = first_sweep(
        wanted, own, payload, atoms, scales, weights, current, integrals, denominator
    )
    amp = lax.all_to_all(amp, both, split_axis=0, concat_axis=0, tiled=True)
    new, residual = second_sweep(mask, cat, weights, amp, current, integrals, denominator)
    return new, residual


def solution(mesh):
    count = mesh.shape["pair"]
    devices = mesh.devices.reshape(mesh.shape["frag"], 2, count // 2)
    split_mesh = Mesh(devices, ("frag", "half", "near"))
    rows = ("frag", "half", "near")
    return jax.shard_map(
        on_device,
        mesh=split_mesh,
        in_specs=(
            P(rows, None), P(rows, None), P(rows, None), P(rows), P(rows, None),
            P(rows), P(rows, None), P(rows, None), P(rows, None, None), P(rows, None),
        ),
        out_specs=(P(rows, None), P(rows, None)),
        check_vma=False,
    )
```

```python
import jax
import jax.numpy as jnp
from jax import lax
from jax.experimental import pallas as pl
from jax.experimental.pallas import tpu as pltpu
from jax.sharding import Mesh, PartitionSpec as P

ATOMS = 32
CHUNK = 4
ONE_STEP = 16
LOG_TOP = 125.0
CODE_TOP = 32767.0
CODE_ROWS = 16
SMALLEST = 2.0**-100
VMEM_LIMIT = 32 * 1024 * 1024
NT = (((1,), (1,)), ((), ()))


def split(value):
    high = value.astype(jnp.bfloat16)
    low = (value - high.astype(jnp.float32)).astype(jnp.bfloat16)
    return high, low


def scale_of(eighths):
    return jnp.exp2(eighths * 0.125)


def eighths_of(value):
    top = jnp.maximum(jnp.max(jnp.abs(value), axis=0, keepdims=True), SMALLEST)
    return jnp.ceil(jnp.log2(top) * 8.0)


def store_codes(value, even_ref, odd_ref, p):
    size = value.shape[0]
    eighths = eighths_of(value)
    codes = jnp.clip(jnp.round(value * (CODE_TOP / scale_of(eighths))), -CODE_TOP, CODE_TOP)
    rows = jnp.concatenate([codes, jnp.broadcast_to(eighths, (CODE_ROWS, size))], axis=0)
    blank = jnp.zeros_like(rows)
    for ref, parts in ((even_ref, [rows, blank]), (odd_ref, [blank, rows])):
        ref[p] = jnp.concatenate(parts, axis=1).astype(jnp.int32).astype(jnp.int16)


def block_of_codes(codes):
    rows = codes.astype(jnp.int32).astype(jnp.float32)
    size = rows.shape[0] - CODE_ROWS
    return rows[:size, :] * (scale_of(rows[size : size + 1, :]) * (1.0 / CODE_TOP))


def log_code(value, eighths):
    power = jnp.clip(value * (LOG_TOP / scale_of(eighths)), -LOG_TOP, LOG_TOP)
    return jnp.exp2(power)


def block_of_logs(first, second, eighths):
    rows, lanes = first.shape[0], eighths.shape[1]
    size = lanes // 2
    left = lax.broadcasted_iota(jnp.int32, (rows, lanes), 1) < size
    quarters = []
    for start in range(0, 2 * lanes, lanes):
        a, b = first[:, start : start + lanes], second[:, start : start + lanes]
        quarters.append(jnp.where(left, a, pltpu.roll(b, size, 1)))
        quarters.append(jnp.where(left, pltpu.roll(a, size, 1), b))
    both = jnp.concatenate(quarters, axis=0)
    return jnp.log2(both) * (scale_of(eighths) * (1.0 / LOG_TOP))


def to_blocks(flat_ref, rows_ref, size):
    pairs = flat_ref.shape[0]
    for a in range(0, size, 2):
        both = flat_ref[:, a * size : (a + 2) * size]
        rows_ref[pl.ds(a, pairs, stride=size), :] = both[:, :size]
        rows_ref[pl.ds(a + 1, pairs, stride=size), :] = both[:, size:]


def atoms_of_columns(domains, width):
    count = domains.shape[1]
    entry = lax.broadcasted_iota(jnp.int32, (count, width), 0)
    column = lax.broadcasted_iota(jnp.int32, (count, width), 1)
    spread = (entry == column // (width // count)).astype(jnp.float32).astype(jnp.bfloat16)
    atoms = domains.astype(jnp.float32).astype(jnp.bfloat16)
    return jnp.dot(atoms, spread, preferred_element_type=jnp.float32)


def column_table(atoms, columns):
    width = atoms.shape[1]
    per_atom = columns // ATOMS
    row = lax.broadcasted_iota(jnp.int32, (columns, width), 0).astype(jnp.int16)
    column = lax.broadcasted_iota(jnp.int32, (1, width), 1)
    ids = (atoms.astype(jnp.int32) * per_atom + column % per_atom).astype(jnp.int16)
    return jnp.where(row == ids, jnp.ones((), jnp.bfloat16), jnp.zeros((), jnp.bfloat16))


def prepare_kernel(
    half_ref, request_ref, table_ref, pnos_ref, domains_ref, amp_ref, integrals_ref, weight_ref,
    position_ref, own_ref, current_ref, blocks_ref, atoms_ref, scales_ref, weights_ref, mask_ref,
    own_atoms_ref, info_ref,
):
    pairs, size, width = pnos_ref.shape
    columns = own_ref.shape[1]
    entries = scales_ref.shape[0]
    half = half_ref[0]
    to_blocks(amp_ref, current_ref, size)
    to_blocks(integrals_ref, blocks_ref, size)
    own_atoms_ref[...] = atoms_of_columns(domains_ref[...], width)
    for p in range(pairs):
        own_ref[p * size : (p + 1) * size, :] = lax.dot_general(
            pnos_ref[p], column_table(own_atoms_ref[p : p + 1, :], columns), NT,
            preferred_element_type=jnp.float32,
        ).astype(jnp.bfloat16)

    count = domains_ref.shape[1]
    lanes = table_ref.shape[2]
    for k in range(2 * entries):
        source = source_of(k // 2, half, entries // 2)
        row = request_ref[0, source * 2 + k % 2]
        info_ref[k : k + 1, :lanes] = table_ref[source, pl.ds(row, 1), :]
    atoms_ref[...] = atoms_of_columns(info_ref[:, size : size + count], width)
    scales = info_ref[:, : 2 * size].astype(jnp.float32)
    moved = pltpu.roll(scales, size, 1)
    left_lanes = lax.broadcasted_iota(jnp.int32, (1, 2 * size), 1) < size
    for e in range(entries):
        scales_ref[e : e + 1, :] = jnp.where(
            left_lanes, scales[2 * e : 2 * e + 1, :], moved[2 * e + 1 : 2 * e + 2, :]
        )
    for c in range(weights_ref.shape[0]):
        weights_ref[c] = slot_weights(
            half, entries // 2, c * CHUNK, weight_ref, position_ref, size
        )
    mask_ref[...] = jnp.full_like(mask_ref, half)


def encode_kernel(
    pnos_hbm, amp_hbm, domains_hbm, request_hbm, pnos_ref, logs_ref, table_ref, amp_ref,
    domains_ref, request_ref, rows_ref, sem_ref,
):
    pairs, size, unused = pnos_hbm.shape
    quarter = logs_ref.shape[1]
    copies = [
        pltpu.make_async_copy(amp_hbm, amp_ref, sem_ref.at[0]),
        pltpu.make_async_copy(domains_hbm, domains_ref, sem_ref.at[1]),
        pltpu.make_async_copy(request_hbm, request_ref, sem_ref.at[2]),
        pltpu.make_async_copy(pnos_hbm, pnos_ref, sem_ref.at[3]),
    ]
    for copy in copies:
        copy.start()
    for copy in copies[:3]:
        copy.wait()
    to_blocks(amp_ref, rows_ref, size)
    scales = []
    for p in range(pairs):
        block = rows_ref[p * size : (p + 1) * size, :]
        eighths = eighths_of(block)
        logs = log_code(block, eighths)
        logs_ref[p] = jnp.concatenate(
            [logs[q : q + quarter, :] for q in range(0, size, quarter)], axis=1
        ).astype(jnp.bfloat16)
        scales.append(eighths)
    scales = jnp.concatenate(scales, axis=0).astype(jnp.int32)
    count = domains_ref.shape[1]
    slots = request_ref.shape[1]
    table_ref[:, :size] = scales
    table_ref[:, size : size + count] = domains_ref[...]
    table_ref[:, size + count :] = jnp.broadcast_to(request_ref[...], (pairs, slots))
    copies[3].wait()


def pack_kernel(
    here_ref, there_ref, pnos_ref, logs_ref, far_pnos_ref, far_logs_ref, out_hbm, sem_ref
):
    unused, size, width = pnos_ref.shape
    quarter = logs_ref.shape[1]

    def pack(n, carry):
        parts = ((here_ref, pnos_ref, logs_ref), (there_ref, far_pnos_ref, far_logs_ref))
        for part, (wanted_ref, blocks_ref, codes_ref) in enumerate(parts):
            for c in range(2):
                pair = wanted_ref[n, c]
                to = out_hbm.at[n, part, c]
                pltpu.make_async_copy(
                    blocks_ref.at[pair], to.at[pl.ds(0, size)], sem_ref.at[0]
                ).start()
                pltpu.make_async_copy(
                    codes_ref.at[pair], to.at[pl.ds(size, quarter)], sem_ref.at[0]
                ).start()
        return carry

    lax.fori_loop(0, out_hbm.shape[0], pack, 0)
    pltpu.make_async_copy(out_hbm, out_hbm, sem_ref.at[0]).wait()


def source_of(entry, half, near):
    return (entry % 2 + half) % 2 * near + entry // 2


def slot_weights(half, near, start, weight_ref, position_ref, size):
    slot = lax.broadcasted_iota(jnp.int32, (1, 2 * CHUNK * size), 1) // size
    source = source_of(start + slot // 2, half, near)
    named = source * 2 + slot % 2
    total = jnp.zeros((weight_ref.shape[0], named.shape[1]), jnp.float32)
    for c in range(weight_ref.shape[1]):
        hit = position_ref[:, c : c + 1] == named
        total += jnp.where(hit, weight_ref[:, c : c + 1], 0.0)
    return total


def half_products(weights, amps, cat_ref, left_ref):
    pairs, rows2, lanes = cat_ref.shape
    size = rows2 // 2
    group = lax.broadcasted_iota(jnp.int32, (size, 4 * size), 1) // size
    even = (group % 2 == 0).astype(jnp.float32).astype(jnp.bfloat16)
    odd = (group % 2 == 1).astype(jnp.float32).astype(jnp.bfloat16)
    for j in range(CHUNK):
        cols = slice(j * 2 * size, (j + 1) * 2 * size)
        amp = jnp.concatenate(split(amps(j)), axis=1)
        first, second = amp * even, amp * odd
        right = jnp.concatenate([first, second, first, second], axis=0)
        high = cat_ref[:, :size, cols].reshape(pairs * size, 2 * size)
        low = cat_ref[:, size:, cols].reshape(pairs * size, 2 * size)
        both = jnp.dot(
            jnp.concatenate([high, low], axis=1), right, preferred_element_type=jnp.float32
        )
        left = (both[:, : 2 * size] + both[:, 2 * size :]).reshape(pairs, size, 2 * size)
        left = left * weights[:, cols].reshape(pairs, 1, 2 * size)
        left_high, left_low = split(left)
        left_ref[:, :size, cols] = left_high
        left_ref[:, size:, cols] = left_low


def add_products(first, cat_ref, left_ref, acc_ref):
    for s in range(acc_ref.shape[0]):
        total = jnp.where(first, 0.0, acc_ref[s])
        for c in range(cat_ref.shape[0]):
            total += lax.dot_general(
                left_ref[c, s], cat_ref[c, s], NT, preferred_element_type=jnp.float32
            )
        acc_ref[s] = total


def cross_chunk(atoms, own_ref, payload_ref, cat_ref, full_ref):
    columns = own_ref.shape[1]
    pairs, rows2, unused = cat_ref.shape
    size = rows2 // 2
    for k in range(2 * CHUNK):
        n, c = k // 2, k % 2
        full_ref[k * size : (k + 1) * size, :] = lax.dot_general(
            payload_ref[n, c, :size, :],
            column_table(atoms[k : k + 1, :], columns), NT, preferred_element_type=jnp.float32,
        ).astype(jnp.bfloat16)
    cross = lax.dot_general(own_ref[...], full_ref[...], NT, preferred_element_type=jnp.float32)
    high, low = split(cross)
    cat_ref[:, :size, :] = high.reshape(pairs, size, -1)
    cat_ref[:, size:, :] = low.reshape(pairs, size, -1)


def coupled_of(acc):
    size = acc.shape[0] // 2
    rows = acc[:size] + acc[size:]
    return rows[:, :size] + rows[:, size:]


def first_kernel(
    wanted_hbm, own_ref, payload_ref, atoms_ref, scales_ref, weights_ref, current_ref,
    integrals_ref, denominator_ref, cat_ref, new_ref, send_hbm, full_ref, left_ref, acc_ref,
    send_ref, even_ref, odd_ref, wanted_ref, sem_ref,
):
    pairs, size, unused = denominator_ref.shape
    chunks = cat_ref.shape[0]
    step = pl.program_id(0)
    wanted_copy = pltpu.make_async_copy(wanted_hbm, wanted_ref, sem_ref.at[0])

    @pl.when(step == 0)
    def fetch():
        wanted_copy.start()

    for c in range(chunks):
        blocks = payload_ref.at[pl.ds(c * CHUNK, CHUNK)]
        chunk = step * chunks + c
        atoms = atoms_ref[pl.ds(chunk * 2 * CHUNK, 2 * CHUNK), :]
        cross_chunk(atoms, own_ref, blocks, cat_ref.at[c], full_ref.at[c])

        def amps(j, chunk=chunk, blocks=blocks):
            eighths = scales_ref[pl.ds(chunk * CHUNK + j, 1), :]
            logs = [blocks[j, i, size:, :].astype(jnp.float32) for i in range(2)]
            return block_of_logs(*logs, eighths)

        half_products(weights_ref[chunk], amps, cat_ref.at[c], left_ref.at[c])
    add_products(step == 0, cat_ref, left_ref, acc_ref)

    @pl.when(step == pl.num_programs(0) - 1)
    def finish():
        for s in range(pairs):
            rows = slice(s * size, (s + 1) * size)
            current, denominator = current_ref[rows, :], denominator_ref[s]
            residual = integrals_ref[rows, :] + denominator * current - coupled_of(acc_ref[s])
            new = current - residual / denominator
            new_ref[rows, :] = new
            store_codes(new, even_ref, odd_ref, s)

        wanted_copy.wait()

        def pack(d, carry):
            send_ref[d] = even_ref[wanted_ref[d, 0]] + odd_ref[wanted_ref[d, 1]]
            return carry

        lax.fori_loop(0, send_ref.shape[0], pack, 0)
        copy = pltpu.make_async_copy(send_ref, send_hbm, sem_ref.at[0])
        copy.start()
        copy.wait()


def second_kernel(
    mask_ref, cat_ref, weights_ref, amp_ref, current_ref, integrals_ref, denominator_ref,
    new_ref, residual_ref, left_ref, acc_ref, new_rows_ref, residual_rows_ref,
):
    pairs, size, unused = denominator_ref.shape
    step = pl.program_id(0)
    near = amp_ref.shape[0] // 2
    chunks = cat_ref.shape[0]
    upper = mask_ref[:1, :] > 0
    for c in range(chunks):
        chunk = step * chunks + c

        def amps(j, chunk=chunk):
            entry = chunk * CHUNK + j
            low = block_of_codes(amp_ref[entry // 2])
            high = block_of_codes(amp_ref[near + entry // 2])
            return jnp.where(upper, low, high) if j % 2 else jnp.where(upper, high, low)

        half_products(weights_ref[chunk], amps, cat_ref.at[c], left_ref.at[c])
    add_products(step == 0, cat_ref, left_ref, acc_ref)

    @pl.when(step == pl.num_programs(0) - 1)
    def finish():
        for s in range(pairs):
            rows = slice(s * size, (s + 1) * size)
            current, denominator = current_ref[rows, :], denominator_ref[s]
            residual = integrals_ref[rows, :] + denominator * current - coupled_of(acc_ref[s])
            residual_rows_ref[rows, :] = residual
            new_rows_ref[rows, :] = current - residual / denominator
        for rows_ref, out_ref in ((residual_rows_ref, residual_ref), (new_rows_ref, new_ref)):
            for a in range(0, size, 2):
                out_ref[:, a * size : (a + 2) * size] = jnp.concatenate(
                    [rows_ref[pl.ds(a + i, pairs, stride=size), :] for i in range(2)], axis=1
                )


def smem():
    return pl.BlockSpec(memory_space=pltpu.SMEM)


def vmem():
    return pl.BlockSpec(memory_space=pltpu.VMEM)


def hbm():
    return pl.BlockSpec(memory_space=pltpu.HBM)


def in_hbm(*arrays):
    return [pltpu.with_memory_space_constraint(array, pltpu.HBM) for array in arrays]


def params():
    return pltpu.CompilerParams(
        dimension_semantics=("arbitrary",), vmem_limit_bytes=VMEM_LIMIT
    )


def limit():
    return pltpu.CompilerParams(vmem_limit_bytes=VMEM_LIMIT)


def prepare(half, request, table, pnos, domains, amplitudes, integrals, weight, position):
    pairs, size, width = pnos.shape
    entries = request.shape[1] // 2
    own = (pairs * size, ATOMS * (width // domains.shape[1]))
    block = (pairs * size, size)
    out = (
        (own, jnp.bfloat16), (block, jnp.float32), (block, jnp.float32),
        ((2 * entries, width), jnp.float32), ((entries, 2 * size), jnp.float32),
        ((entries // CHUNK, pairs, 2 * CHUNK * size), jnp.float32), ((8, 2 * size), jnp.int32),
    )
    return pl.pallas_call(
        prepare_kernel,
        in_specs=[smem()] * 2 + [vmem()] * 7,
        out_specs=[vmem()] * len(out),
        out_shape=[jax.ShapeDtypeStruct(shape, dtype) for shape, dtype in out],
        scratch_shapes=[
            pltpu.VMEM((pairs, width), jnp.float32),
            pltpu.VMEM((2 * entries, max(table.shape[2], 2 * size)), jnp.int32),
        ],
        compiler_params=limit(),
        name="prepare",
    )(half, request, table, pnos, domains, amplitudes, integrals, weight, position)


def encode(pnos, amplitudes, domains, request):
    pairs, size, width = pnos.shape
    quarter = size * size // width
    lanes = size + domains.shape[1] + request.shape[1]
    return pl.pallas_call(
        encode_kernel,
        in_specs=[hbm()] * 4,
        out_specs=[vmem()] * 3,
        out_shape=[
            jax.ShapeDtypeStruct(pnos.shape, jnp.bfloat16),
            jax.ShapeDtypeStruct((pairs, quarter, width), jnp.bfloat16),
            jax.ShapeDtypeStruct((pairs, lanes), jnp.int32),
        ],
        scratch_shapes=[
            pltpu.VMEM(amplitudes.shape, jnp.float32), pltpu.VMEM(domains.shape, jnp.int32),
            pltpu.VMEM(request.shape, jnp.int32), pltpu.VMEM((pairs * size, size), jnp.float32),
            pltpu.SemaphoreType.DMA((4,)),
        ],
        compiler_params=limit(),
        name="encode",
    )(*in_hbm(pnos, amplitudes, domains, request))


def pack_payload(here, there, pnos, logs, far_pnos, far_logs):
    unused, size, width = pnos.shape
    out = (here.shape[0], 2, 2, size + logs.shape[1], width)
    return pl.pallas_call(
        pack_kernel,
        in_specs=[smem(), smem()] + [vmem()] * 4,
        out_specs=hbm(),
        out_shape=pltpu.HBM(out, pnos.dtype),
        scratch_shapes=[pltpu.SemaphoreType.DMA((1,))],
        compiler_params=limit(),
        name="pack_payload",
    )(here, there, pnos, logs, far_pnos, far_logs)


def sweep_shapes(entries, pairs, size):
    chunks = entries // CHUNK if entries <= ONE_STEP else 1
    cat = (entries // CHUNK, pairs, 2 * size, 2 * CHUNK * size)
    held = (chunks,) + cat[1:]
    scratch = [
        pltpu.VMEM(held, jnp.bfloat16), pltpu.VMEM(held, jnp.bfloat16),
        pltpu.VMEM((pairs, 2 * size, 2 * size), jnp.float32),
    ]
    return cat[0] // chunks, chunks, cat, scratch


def cat_spec(steps, chunks, cat):
    if steps == 1:
        return vmem()
    return pl.BlockSpec((chunks,) + cat[1:], lambda i: (i, 0, 0, 0))


def first_sweep(
    wanted, own, payload, atoms, scales, weights, current, integrals, denominator
):
    pairs, size, unused = denominator.shape
    entries = payload.shape[0]
    steps, chunks, cat, (cats, lefts, acc) = sweep_shapes(entries, pairs, size)
    block = (CHUNK * chunks,) + payload.shape[1:]
    blocks = vmem() if steps == 1 else pl.BlockSpec(block, lambda i: (i, 0, 0, 0))
    kept = cat_spec(steps, chunks, cat)
    parts = (pairs, size + CODE_ROWS, 2 * size)
    send = (entries,) + parts[1:]
    return pl.pallas_call(
        first_kernel,
        grid=(steps,),
        in_specs=[hbm(), vmem(), blocks] + [vmem()] * 6,
        out_specs=[kept, vmem(), hbm()],
        out_shape=[
            jax.ShapeDtypeStruct(cat, jnp.bfloat16),
            jax.ShapeDtypeStruct(current.shape, jnp.float32),
            pltpu.HBM(send, jnp.int16),
        ],
        scratch_shapes=[
            pltpu.VMEM((chunks, cat[3], own.shape[1]), jnp.bfloat16),
            lefts,
            acc,
            pltpu.VMEM(send, jnp.int16),
            pltpu.VMEM(parts, jnp.int16),
            pltpu.VMEM(parts, jnp.int16),
            pltpu.SMEM(wanted.shape, jnp.int32),
            pltpu.SemaphoreType.DMA((1,)),
        ],
        compiler_params=params(),
        name="first_sweep",
    )(
        *in_hbm(wanted), own, payload, atoms, scales, weights, current, integrals, denominator
    )


def second_sweep(mask, cat, weights, amp, current, integrals, denominator):
    pairs, size, unused = denominator.shape
    steps, chunks, shape, scratch = sweep_shapes(amp.shape[0], pairs, size)
    flat = (pairs, size * size)
    return pl.pallas_call(
        second_kernel,
        grid=(steps,),
        in_specs=[vmem(), cat_spec(steps, chunks, shape)] + [vmem()] * 5,
        out_specs=[vmem(), vmem()],
        out_shape=[jax.ShapeDtypeStruct(flat, jnp.float32)] * 2,
        scratch_shapes=scratch[1:] + [
            pltpu.VMEM(current.shape, jnp.float32),
            pltpu.VMEM(current.shape, jnp.float32),
        ],
        compiler_params=params(),
        name="second_sweep",
    )(
        mask, cat, weights, amp, current, integrals, denominator
    )


def on_device(
    amplitudes, integrals, virtual, occupied, coupling, degree, position, request, pnos, domains
):
    pairs = amplitudes.shape[0]
    size = virtual.shape[1]
    depth = coupling.shape[1]
    slots = request.shape[1]
    entries = slots // 2
    near = entries // 2
    half = lax.axis_index("half").astype(jnp.int32)
    mine = lax.axis_index("near").astype(jnp.int32)
    swap = [(0, 1), (1, 0)]
    both = ("half", "near")

    far_pnos = lax.ppermute(pnos, "half", swap)
    near_pnos, logs, table = encode(pnos, amplitudes, domains, request)
    far_logs = lax.ppermute(logs, "half", swap)

    table = jnp.broadcast_to(table[None], (entries,) + table.shape)
    table = lax.all_to_all(table, both, split_axis=0, concat_axis=0, tiled=True)
    column = table.shape[2] - slots + 2 * mine
    wanted = lax.dynamic_slice(
        table, (0, 0, column + half * 2 * near), (entries, 1, 2)
    ).reshape(entries, 2)
    here = lax.dynamic_slice(wanted, (half * near, 0), (near, 2))
    there = lax.dynamic_slice(
        table, (half * near, 0, column + (1 - half) * 2 * near), (near, 1, 2)
    ).reshape(near, 2)

    payload = pack_payload(here, there, near_pnos, logs, far_pnos, far_logs)
    payload = lax.all_to_all(payload, "near", split_axis=0, concat_axis=0, tiled=True)
    payload = payload.reshape((entries,) + payload.shape[2:])

    live = jnp.arange(depth, dtype=jnp.int32)[None, :] < degree[:, None]
    weight = jnp.where(live, coupling, jnp.zeros_like(coupling))
    denominator = virtual[:, :, None] + virtual[:, None, :] - occupied[:, None, None]
    own, current, integrals, atoms, scales, weights, mask = prepare(
        half.reshape(1), request, table, pnos, domains, amplitudes, integrals, weight, position
    )
    cat, current, amp = first_sweep(
        wanted, own, payload, atoms, scales, weights, current, integrals, denominator
    )
    amp = lax.all_to_all(amp, both, split_axis=0, concat_axis=0, tiled=True)
    new, residual = second_sweep(mask, cat, weights, amp, current, integrals, denominator)
    return new, residual


def solution(mesh):
    count = mesh.shape["pair"]
    devices = mesh.devices.reshape(mesh.shape["frag"], 2, count // 2)
    split_mesh = Mesh(devices, ("frag", "half", "near"))
    rows = ("frag", "half", "near")
    return jax.shard_map(
        on_device,
        mesh=split_mesh,
        in_specs=(
            P(rows, None), P(rows, None), P(rows, None), P(rows), P(rows, None),
            P(rows), P(rows, None), P(rows, None), P(rows, None, None), P(rows, None),
        ),
        out_specs=(P(rows, None), P(rows, None)),
        check_vma=False,
    )
```

```python
import jax
import jax.numpy as jnp
from jax import lax
from jax.experimental import pallas as pl
from jax.experimental.pallas import tpu as pltpu
from jax.sharding import Mesh, PartitionSpec as P

ATOMS = 32
CHUNK = 4
ONE_STEP = 16
LOG_TOP = 125.0
CODE_TOP = 32767.0
CODE_ROWS = 16
SMALLEST = 2.0**-100
VMEM_LIMIT = 32 * 1024 * 1024
NT = (((1,), (1,)), ((), ()))


def split(value):
    high = value.astype(jnp.bfloat16)
    low = (value - high.astype(jnp.float32)).astype(jnp.bfloat16)
    return high, low


def scale_of(eighths):
    return jnp.exp2(eighths * 0.125)


def eighths_of(value):
    top = jnp.maximum(jnp.max(jnp.abs(value), axis=0, keepdims=True), SMALLEST)
    return jnp.ceil(jnp.log2(top) * 8.0)


def store_codes(value, even_ref, odd_ref, p):
    size = value.shape[0]
    eighths = eighths_of(value)
    codes = jnp.clip(jnp.round(value * (CODE_TOP / scale_of(eighths))), -CODE_TOP, CODE_TOP)
    rows = jnp.concatenate([codes, jnp.broadcast_to(eighths, (CODE_ROWS, size))], axis=0)
    blank = jnp.zeros_like(rows)
    for ref, parts in ((even_ref, [rows, blank]), (odd_ref, [blank, rows])):
        ref[p] = jnp.concatenate(parts, axis=1).astype(jnp.int32).astype(jnp.int16)


def block_of_codes(codes):
    rows = codes.astype(jnp.int32).astype(jnp.float32)
    size = rows.shape[0] - CODE_ROWS
    return rows[:size, :] * (scale_of(rows[size : size + 1, :]) * (1.0 / CODE_TOP))


def log_code(value, eighths):
    power = jnp.clip(value * (LOG_TOP / scale_of(eighths)), -LOG_TOP, LOG_TOP)
    return jnp.exp2(power)


def block_of_logs(first, second, eighths):
    rows, lanes = first.shape[0], eighths.shape[1]
    size = lanes // 2
    left = lax.broadcasted_iota(jnp.int32, (rows, lanes), 1) < size
    quarters = []
    for start in range(0, 2 * lanes, lanes):
        a, b = first[:, start : start + lanes], second[:, start : start + lanes]
        quarters.append(jnp.where(left, a, pltpu.roll(b, size, 1)))
        quarters.append(jnp.where(left, pltpu.roll(a, size, 1), b))
    both = jnp.concatenate(quarters, axis=0)
    return jnp.log2(both) * (scale_of(eighths) * (1.0 / LOG_TOP))


def to_blocks(flat_ref, rows_ref, size):
    pairs = flat_ref.shape[0]
    for a in range(0, size, 2):
        both = flat_ref[:, a * size : (a + 2) * size]
        rows_ref[pl.ds(a, pairs, stride=size), :] = both[:, :size]
        rows_ref[pl.ds(a + 1, pairs, stride=size), :] = both[:, size:]


def atoms_of_columns(domains, width):
    count = domains.shape[1]
    entry = lax.broadcasted_iota(jnp.int32, (count, width), 0)
    column = lax.broadcasted_iota(jnp.int32, (count, width), 1)
    spread = (entry == column // (width // count)).astype(jnp.float32).astype(jnp.bfloat16)
    atoms = domains.astype(jnp.float32).astype(jnp.bfloat16)
    return jnp.dot(atoms, spread, preferred_element_type=jnp.float32)


def column_table(atoms, columns):
    width = atoms.shape[1]
    per_atom = columns // ATOMS
    row = lax.broadcasted_iota(jnp.int32, (columns, width), 0).astype(jnp.int16)
    column = lax.broadcasted_iota(jnp.int32, (1, width), 1)
    ids = (atoms.astype(jnp.int32) * per_atom + column % per_atom).astype(jnp.int16)
    return jnp.where(row == ids, jnp.ones((), jnp.bfloat16), jnp.zeros((), jnp.bfloat16))


def prepare_kernel(
    half_ref, request_ref, table_ref, pnos_ref, domains_ref, amp_ref, integrals_ref, weight_ref,
    position_ref, own_ref, current_ref, blocks_ref, atoms_ref, scales_ref, weights_ref, mask_ref,
    own_atoms_ref, info_ref,
):
    pairs, size, width = pnos_ref.shape
    columns = own_ref.shape[1]
    entries = scales_ref.shape[0]
    half = half_ref[0]
    to_blocks(amp_ref, current_ref, size)
    to_blocks(integrals_ref, blocks_ref, size)
    own_atoms_ref[...] = atoms_of_columns(domains_ref[...], width)
    for p in range(pairs):
        own_ref[p * size : (p + 1) * size, :] = lax.dot_general(
            pnos_ref[p], column_table(own_atoms_ref[p : p + 1, :], columns), NT,
            preferred_element_type=jnp.float32,
        ).astype(jnp.bfloat16)

    count = domains_ref.shape[1]
    lanes = table_ref.shape[2]
    for k in range(2 * entries):
        source = source_of(k // 2, half, entries // 2)
        row = request_ref[0, source * 2 + k % 2]
        info_ref[k : k + 1, :lanes] = table_ref[source, pl.ds(row, 1), :]
    atoms_ref[...] = atoms_of_columns(info_ref[:, size : size + count], width)
    scales = info_ref[:, : 2 * size].astype(jnp.float32)
    moved = pltpu.roll(scales, size, 1)
    left_lanes = lax.broadcasted_iota(jnp.int32, (1, 2 * size), 1) < size
    for e in range(entries):
        scales_ref[e : e + 1, :] = jnp.where(
            left_lanes, scales[2 * e : 2 * e + 1, :], moved[2 * e + 1 : 2 * e + 2, :]
        )
    for c in range(weights_ref.shape[0]):
        weights_ref[c] = slot_weights(
            half, entries // 2, c * CHUNK, weight_ref, position_ref, size
        )
    mask_ref[...] = jnp.full_like(mask_ref, half)


def encode_kernel(
    pnos_hbm, amp_hbm, domains_hbm, request_hbm, pnos_ref, logs_ref, table_ref, amp_ref,
    domains_ref, request_ref, rows_ref, sem_ref,
):
    pairs, size, unused = pnos_hbm.shape
    quarter = logs_ref.shape[1]
    copies = [
        pltpu.make_async_copy(amp_hbm, amp_ref, sem_ref.at[0]),
        pltpu.make_async_copy(domains_hbm, domains_ref, sem_ref.at[1]),
        pltpu.make_async_copy(request_hbm, request_ref, sem_ref.at[2]),
        pltpu.make_async_copy(pnos_hbm, pnos_ref, sem_ref.at[3]),
    ]
    for copy in copies:
        copy.start()
    for copy in copies[:3]:
        copy.wait()
    to_blocks(amp_ref, rows_ref, size)
    scales = []
    for p in range(pairs):
        block = rows_ref[p * size : (p + 1) * size, :]
        eighths = eighths_of(block)
        logs = log_code(block, eighths)
        logs_ref[p] = jnp.concatenate(
            [logs[q : q + quarter, :] for q in range(0, size, quarter)], axis=1
        ).astype(jnp.bfloat16)
        scales.append(eighths)
    scales = jnp.concatenate(scales, axis=0).astype(jnp.int32)
    count = domains_ref.shape[1]
    slots = request_ref.shape[1]
    table_ref[:, :size] = scales
    table_ref[:, size : size + count] = domains_ref[...]
    table_ref[:, size + count :] = jnp.broadcast_to(request_ref[...], (pairs, slots))
    copies[3].wait()


def pack_kernel(
    here_ref, there_ref, pnos_ref, logs_ref, far_pnos_ref, far_logs_ref, out_hbm, sem_ref
):
    unused, size, width = pnos_ref.shape
    quarter = logs_ref.shape[1]

    def pack(n, carry):
        parts = ((here_ref, pnos_ref, logs_ref), (there_ref, far_pnos_ref, far_logs_ref))
        for part, (wanted_ref, blocks_ref, codes_ref) in enumerate(parts):
            for c in range(2):
                pair = wanted_ref[n, c]
                to = out_hbm.at[n, part, c]
                pltpu.make_async_copy(
                    blocks_ref.at[pair], to.at[pl.ds(0, size)], sem_ref.at[0]
                ).start()
                pltpu.make_async_copy(
                    codes_ref.at[pair], to.at[pl.ds(size, quarter)], sem_ref.at[0]
                ).start()
        return carry

    lax.fori_loop(0, out_hbm.shape[0], pack, 0)
    pltpu.make_async_copy(out_hbm, out_hbm, sem_ref.at[0]).wait()


def source_of(entry, half, near):
    return (entry % 2 + half) % 2 * near + entry // 2


def slot_weights(half, near, start, weight_ref, position_ref, size):
    slot = lax.broadcasted_iota(jnp.int32, (1, 2 * CHUNK * size), 1) // size
    source = source_of(start + slot // 2, half, near)
    named = source * 2 + slot % 2
    total = jnp.zeros((weight_ref.shape[0], named.shape[1]), jnp.float32)
    for c in range(weight_ref.shape[1]):
        hit = position_ref[:, c : c + 1] == named
        total += jnp.where(hit, weight_ref[:, c : c + 1], 0.0)
    return total


def half_products(weights, amps, cat_ref, left_ref):
    pairs, rows2, lanes = cat_ref.shape
    size = rows2 // 2
    group = lax.broadcasted_iota(jnp.int32, (size, 4 * size), 1) // size
    even = (group % 2 == 0).astype(jnp.float32).astype(jnp.bfloat16)
    odd = (group % 2 == 1).astype(jnp.float32).astype(jnp.bfloat16)
    for j in range(CHUNK):
        cols = slice(j * 2 * size, (j + 1) * 2 * size)
        amp = jnp.concatenate(split(amps(j)), axis=1)
        first, second = amp * even, amp * odd
        right = jnp.concatenate([first, second, first, second], axis=0)
        high = cat_ref[:, :size, cols].reshape(pairs * size, 2 * size)
        low = cat_ref[:, size:, cols].reshape(pairs * size, 2 * size)
        both = jnp.dot(
            jnp.concatenate([high, low], axis=1), right, preferred_element_type=jnp.float32
        )
        left = (both[:, : 2 * size] + both[:, 2 * size :]).reshape(pairs, size, 2 * size)
        left = left * weights[:, cols].reshape(pairs, 1, 2 * size)
        left_high, left_low = split(left)
        left_ref[:, :size, cols] = left_high
        left_ref[:, size:, cols] = left_low


def add_products(first, cat_ref, left_ref, acc_ref):
    for s in range(acc_ref.shape[0]):
        total = jnp.where(first, 0.0, acc_ref[s])
        for c in range(cat_ref.shape[0]):
            total += lax.dot_general(
                left_ref[c, s], cat_ref[c, s], NT, preferred_element_type=jnp.float32
            )
        acc_ref[s] = total


def cross_chunk(atoms, own_ref, payload_ref, cat_ref, full_ref):
    columns = own_ref.shape[1]
    pairs, rows2, unused = cat_ref.shape
    size = rows2 // 2
    for k in range(2 * CHUNK):
        n, c = k // 2, k % 2
        full_ref[k * size : (k + 1) * size, :] = lax.dot_general(
            payload_ref[n, c, :size, :],
            column_table(atoms[k : k + 1, :], columns), NT, preferred_element_type=jnp.float32,
        ).astype(jnp.bfloat16)
    cross = lax.dot_general(own_ref[...], full_ref[...], NT, preferred_element_type=jnp.float32)
    high, low = split(cross)
    cat_ref[:, :size, :] = high.reshape(pairs, size, -1)
    cat_ref[:, size:, :] = low.reshape(pairs, size, -1)


def coupled_of(acc):
    size = acc.shape[0] // 2
    rows = acc[:size] + acc[size:]
    return rows[:, :size] + rows[:, size:]


def first_kernel(
    wanted_hbm, own_ref, payload_ref, atoms_ref, scales_ref, weights_ref, current_ref,
    integrals_ref, denominator_ref, cat_ref, new_ref, send_hbm, full_ref, left_ref, acc_ref,
    send_ref, even_ref, odd_ref, wanted_ref, sem_ref,
):
    pairs, size, unused = denominator_ref.shape
    chunks = cat_ref.shape[0]
    step = pl.program_id(0)
    wanted_copy = pltpu.make_async_copy(wanted_hbm, wanted_ref, sem_ref.at[0])

    @pl.when(step == 0)
    def fetch():
        wanted_copy.start()

    for c in range(chunks):
        blocks = payload_ref.at[pl.ds(c * CHUNK, CHUNK)]
        chunk = step * chunks + c
        atoms = atoms_ref[pl.ds(chunk * 2 * CHUNK, 2 * CHUNK), :]
        cross_chunk(atoms, own_ref, blocks, cat_ref.at[c], full_ref.at[c])

        def amps(j, chunk=chunk, blocks=blocks):
            eighths = scales_ref[pl.ds(chunk * CHUNK + j, 1), :]
            logs = [blocks[j, i, size:, :].astype(jnp.float32) for i in range(2)]
            return block_of_logs(*logs, eighths)

        half_products(weights_ref[chunk], amps, cat_ref.at[c], left_ref.at[c])
    add_products(step == 0, cat_ref, left_ref, acc_ref)

    @pl.when(step == pl.num_programs(0) - 1)
    def finish():
        for s in range(pairs):
            rows = slice(s * size, (s + 1) * size)
            current, denominator = current_ref[rows, :], denominator_ref[s]
            residual = integrals_ref[rows, :] + denominator * current - coupled_of(acc_ref[s])
            new = current - residual / denominator
            new_ref[rows, :] = new
            store_codes(new, even_ref, odd_ref, s)

        wanted_copy.wait()

        def pack(d, carry):
            send_ref[d] = even_ref[wanted_ref[d, 0]] + odd_ref[wanted_ref[d, 1]]
            return carry

        lax.fori_loop(0, send_ref.shape[0], pack, 0)
        copy = pltpu.make_async_copy(send_ref, send_hbm, sem_ref.at[0])
        copy.start()
        copy.wait()


def second_kernel(
    mask_ref, cat_ref, weights_ref, amp_ref, current_ref, integrals_ref, denominator_ref,
    new_ref, residual_ref, left_ref, acc_ref, new_rows_ref, residual_rows_ref,
):
    pairs, size, unused = denominator_ref.shape
    step = pl.program_id(0)
    near = amp_ref.shape[0] // 2
    chunks = cat_ref.shape[0]
    upper = mask_ref[:1, :] > 0
    for c in range(chunks):
        chunk = step * chunks + c

        def amps(j, chunk=chunk):
            entry = chunk * CHUNK + j
            low = block_of_codes(amp_ref[entry // 2])
            high = block_of_codes(amp_ref[near + entry // 2])
            return jnp.where(upper, low, high) if j % 2 else jnp.where(upper, high, low)

        half_products(weights_ref[chunk], amps, cat_ref.at[c], left_ref.at[c])
    add_products(step == 0, cat_ref, left_ref, acc_ref)

    @pl.when(step == pl.num_programs(0) - 1)
    def finish():
        for s in range(pairs):
            rows = slice(s * size, (s + 1) * size)
            current, denominator = current_ref[rows, :], denominator_ref[s]
            residual = integrals_ref[rows, :] + denominator * current - coupled_of(acc_ref[s])
            residual_rows_ref[rows, :] = residual
            new_rows_ref[rows, :] = current - residual / denominator
        for rows_ref, out_ref in ((residual_rows_ref, residual_ref), (new_rows_ref, new_ref)):
            for a in range(0, size, 2):
                out_ref[:, a * size : (a + 2) * size] = jnp.concatenate(
                    [rows_ref[pl.ds(a + i, pairs, stride=size), :] for i in range(2)], axis=1
                )


def smem():
    return pl.BlockSpec(memory_space=pltpu.SMEM)


def vmem():
    return pl.BlockSpec(memory_space=pltpu.VMEM)


def hbm():
    return pl.BlockSpec(memory_space=pltpu.HBM)


def in_hbm(*arrays):
    return [pltpu.with_memory_space_constraint(array, pltpu.HBM) for array in arrays]


def params():
    return pltpu.CompilerParams(
        dimension_semantics=("arbitrary",), vmem_limit_bytes=VMEM_LIMIT
    )


def limit():
    return pltpu.CompilerParams(vmem_limit_bytes=VMEM_LIMIT)


def prepare(half, request, table, pnos, domains, amplitudes, integrals, weight, position):
    pairs, size, width = pnos.shape
    entries = request.shape[1] // 2
    own = (pairs * size, ATOMS * (width // domains.shape[1]))
    block = (pairs * size, size)
    out = (
        (own, jnp.bfloat16), (block, jnp.float32), (block, jnp.float32),
        ((2 * entries, width), jnp.float32), ((entries, 2 * size), jnp.float32),
        ((entries // CHUNK, pairs, 2 * CHUNK * size), jnp.float32), ((8, 2 * size), jnp.int32),
    )
    return pl.pallas_call(
        prepare_kernel,
        in_specs=[smem()] * 2 + [vmem()] * 7,
        out_specs=[vmem()] * len(out),
        out_shape=[jax.ShapeDtypeStruct(shape, dtype) for shape, dtype in out],
        scratch_shapes=[
            pltpu.VMEM((pairs, width), jnp.float32),
            pltpu.VMEM((2 * entries, max(table.shape[2], 2 * size)), jnp.int32),
        ],
        compiler_params=limit(),
        name="prepare",
    )(half, request, table, pnos, domains, amplitudes, integrals, weight, position)


def encode(pnos, amplitudes, domains, request):
    pairs, size, width = pnos.shape
    quarter = size * size // width
    lanes = size + domains.shape[1] + request.shape[1]
    return pl.pallas_call(
        encode_kernel,
        in_specs=[hbm()] * 4,
        out_specs=[vmem()] * 3,
        out_shape=[
            jax.ShapeDtypeStruct(pnos.shape, jnp.bfloat16),
            jax.ShapeDtypeStruct((pairs, quarter, width), jnp.bfloat16),
            jax.ShapeDtypeStruct((pairs, lanes), jnp.int32),
        ],
        scratch_shapes=[
            pltpu.VMEM(amplitudes.shape, jnp.float32), pltpu.VMEM(domains.shape, jnp.int32),
            pltpu.VMEM(request.shape, jnp.int32), pltpu.VMEM((pairs * size, size), jnp.float32),
            pltpu.SemaphoreType.DMA((4,)),
        ],
        compiler_params=limit(),
        name="encode",
    )(*in_hbm(pnos, amplitudes, domains, request))


def pack_payload(here, there, pnos, logs, far_pnos, far_logs):
    unused, size, width = pnos.shape
    out = (here.shape[0], 2, 2, size + logs.shape[1], width)
    return pl.pallas_call(
        pack_kernel,
        in_specs=[smem(), smem()] + [vmem()] * 4,
        out_specs=hbm(),
        out_shape=pltpu.HBM(out, pnos.dtype),
        scratch_shapes=[pltpu.SemaphoreType.DMA((1,))],
        compiler_params=limit(),
        name="pack_payload",
    )(here, there, pnos, logs, far_pnos, far_logs)


def sweep_shapes(entries, pairs, size):
    chunks = entries // CHUNK if entries <= ONE_STEP else 1
    cat = (entries // CHUNK, pairs, 2 * size, 2 * CHUNK * size)
    held = (chunks,) + cat[1:]
    scratch = [
        pltpu.VMEM(held, jnp.bfloat16), pltpu.VMEM(held, jnp.bfloat16),
        pltpu.VMEM((pairs, 2 * size, 2 * size), jnp.float32),
    ]
    return cat[0] // chunks, chunks, cat, scratch


def cat_spec(steps, chunks, cat):
    if steps == 1:
        return vmem()
    return pl.BlockSpec((chunks,) + cat[1:], lambda i: (i, 0, 0, 0))


def first_sweep(
    wanted, own, payload, atoms, scales, weights, current, integrals, denominator
):
    pairs, size, unused = denominator.shape
    entries = payload.shape[0]
    steps, chunks, cat, (cats, lefts, acc) = sweep_shapes(entries, pairs, size)
    block = (CHUNK * chunks,) + payload.shape[1:]
    blocks = vmem() if steps == 1 else pl.BlockSpec(block, lambda i: (i, 0, 0, 0))
    kept = cat_spec(steps, chunks, cat)
    parts = (pairs, size + CODE_ROWS, 2 * size)
    send = (entries,) + parts[1:]
    return pl.pallas_call(
        first_kernel,
        grid=(steps,),
        in_specs=[hbm(), vmem(), blocks] + [vmem()] * 6,
        out_specs=[kept, vmem(), hbm()],
        out_shape=[
            jax.ShapeDtypeStruct(cat, jnp.bfloat16),
            jax.ShapeDtypeStruct(current.shape, jnp.float32),
            pltpu.HBM(send, jnp.int16),
        ],
        scratch_shapes=[
            pltpu.VMEM((chunks, cat[3], own.shape[1]), jnp.bfloat16),
            lefts,
            acc,
            pltpu.VMEM(send, jnp.int16),
            pltpu.VMEM(parts, jnp.int16),
            pltpu.VMEM(parts, jnp.int16),
            pltpu.SMEM(wanted.shape, jnp.int32),
            pltpu.SemaphoreType.DMA((1,)),
        ],
        compiler_params=params(),
        name="first_sweep",
    )(
        *in_hbm(wanted), own, payload, atoms, scales, weights, current, integrals, denominator
    )


def second_sweep(mask, cat, weights, amp, current, integrals, denominator):
    pairs, size, unused = denominator.shape
    steps, chunks, shape, scratch = sweep_shapes(amp.shape[0], pairs, size)
    flat = (pairs, size * size)
    return pl.pallas_call(
        second_kernel,
        grid=(steps,),
        in_specs=[vmem(), cat_spec(steps, chunks, shape)] + [vmem()] * 5,
        out_specs=[vmem(), vmem()],
        out_shape=[jax.ShapeDtypeStruct(flat, jnp.float32)] * 2,
        scratch_shapes=scratch[1:] + [
            pltpu.VMEM(current.shape, jnp.float32),
            pltpu.VMEM(current.shape, jnp.float32),
        ],
        compiler_params=params(),
        name="second_sweep",
    )(
        mask, cat, weights, amp, current, integrals, denominator
    )


def on_device(
    amplitudes, integrals, virtual, occupied, coupling, degree, position, request, pnos, domains
):
    pairs = amplitudes.shape[0]
    size = virtual.shape[1]
    depth = coupling.shape[1]
    slots = request.shape[1]
    entries = slots // 2
    near = entries // 2
    half = lax.axis_index("half").astype(jnp.int32)
    mine = lax.axis_index("near").astype(jnp.int32)
    swap = [(0, 1), (1, 0)]
    both = ("half", "near")

    far_pnos = lax.ppermute(pnos, "half", swap)
    near_pnos, logs, table = encode(pnos, amplitudes, domains, request)
    far_logs = lax.ppermute(logs, "half", swap)

    table = jnp.broadcast_to(table[None].astype(jnp.int16), (entries,) + table.shape)
    table = lax.all_to_all(table, both, split_axis=0, concat_axis=0, tiled=True)
    table = table.astype(jnp.int32)
    column = table.shape[2] - slots + 2 * mine
    wanted = lax.dynamic_slice(
        table, (0, 0, column + half * 2 * near), (entries, 1, 2)
    ).reshape(entries, 2)
    here = lax.dynamic_slice(wanted, (half * near, 0), (near, 2))
    there = lax.dynamic_slice(
        table, (half * near, 0, column + (1 - half) * 2 * near), (near, 1, 2)
    ).reshape(near, 2)

    payload = pack_payload(here, there, near_pnos, logs, far_pnos, far_logs)
    payload = lax.all_to_all(payload, "near", split_axis=0, concat_axis=0, tiled=True)
    payload = payload.reshape((entries,) + payload.shape[2:])

    live = jnp.arange(depth, dtype=jnp.int32)[None, :] < degree[:, None]
    weight = jnp.where(live, coupling, jnp.zeros_like(coupling))
    denominator = virtual[:, :, None] + virtual[:, None, :] - occupied[:, None, None]
    own, current, integrals, atoms, scales, weights, mask = prepare(
        half.reshape(1), request, table, pnos, domains, amplitudes, integrals, weight, position
    )
    cat, current, amp = first_sweep(
        wanted, own, payload, atoms, scales, weights, current, integrals, denominator
    )
    amp = lax.all_to_all(amp, both, split_axis=0, concat_axis=0, tiled=True)
    new, residual = second_sweep(mask, cat, weights, amp, current, integrals, denominator)
    return new, residual


def solution(mesh):
    count = mesh.shape["pair"]
    devices = mesh.devices.reshape(mesh.shape["frag"], 2, count // 2)
    split_mesh = Mesh(devices, ("frag", "half", "near"))
    rows = ("frag", "half", "near")
    return jax.shard_map(
        on_device,
        mesh=split_mesh,
        in_specs=(
            P(rows, None), P(rows, None), P(rows, None), P(rows), P(rows, None),
            P(rows), P(rows, None), P(rows, None), P(rows, None, None), P(rows, None),
        ),
        out_specs=(P(rows, None), P(rows, None)),
        check_vma=False,
    )
```
